256 devices in a mesh: dp: 16 (over z, x_hi), tensor: 16 (over y, x_lo, core).
Axes of the slice: x: 4 (x_hi: 2, x_lo: 2; x = x_hi * 2 + x_lo), y: 4, z: 8, core: 2. Of those that a mesh axis runs over, the one named last changes fastest.
Arguments:
- tokens: bfloat16 [8192, 6144], P('dp', 'tensor'), may hold values from -24 to 24
- upstream: bfloat16 [8192, 24576], P('dp', 'tensor'), may hold values from -0.15625 to 0.15625
- master_weights: float32 [128, 960, 128], P('dp', 'tensor'), may hold values from -0.03 to 0.03
- first_moment: float32 [128, 960, 128], P('dp', 'tensor'), may hold values from -0.5 to 0.5
- second_moment: float32 [128, 960, 128], P('dp', 'tensor'), may hold values from 0.05 to 0.5
- old_blocks: int32 [16, 60], replicated, may hold values from 0 to 9215, as said below
- new_blocks: int32 [16, 60], replicated, may hold values from 0 to 9215, as said below
- new_columns: int32 [16, 12], replicated, may hold values from 0 to 191, as said below
Outputs:
- hidden_out: bfloat16 [8192, 24576], P('dp', 'tensor')
- master_out: float32 [128, 960, 128], P('dp', 'tensor')
- first_out: float32 [128, 960, 128], P('dp', 'tensor')
- second_out: float32 [128, 960, 128], P('dp', 'tensor')
- weight_copy: bfloat16 [128, 960, 128], P(None, 'tensor')
The draws below stay inside these ranges and needn't reach their ends.
Inputs may be any that keep to these rules, and one draw needn't show every extreme that they name: `old_blocks`: row i lists the 60 blocks owner i holds before the reset, in no particular order: all blocks of 12 block columns, 5 in each column; every block number appears at most once in the whole array and the owners' column sets are disjoint and cover all 192 columns. `new_blocks`: row i lists the 60 blocks owner i holds after the reset, in no particular order: all blocks of the columns new_columns[i]. Each column keeps 3 of its old blocks and gains from 0 to 4 blocks that were not there before, 2 a column on average over each owner's columns; every block number appears at most once. `new_columns`: row i lists owner i's 12 block columns after the reset, in the order in which they stand in upstream and hidden_out; every column once. Each owner hands 6 of its former columns to 6 different owners and receives 6 columns from 6 different owners, so between two owners exactly 3 surviving blocks or none change hands.
All inputs are finite; a program needn't handle non-finite values.
Results may differ from the reference program's by a relative error of at most 0.005.
Values may be sent and summed in bfloat16 or wider, within the bound.
No kernel may reach another device: no remote copies, remote signals or barrier semaphores. Data moves between devices by JAX's collectives and lax.ppermute only.
A program may use at most 128 MiB of HBM per device.

```python
import math
import jax
import jax.numpy as jnp
from jax import lax

D = 6144
FF = 24576
B = 128
KB = 5
DROP = 2
STEP = 20
TOKENS = 8192
NBR = 48
NBC = 192
CPD = 12
CAP = 60
SWAP = 6
N_TENSOR = 16


def layout(key):
    rows_count = D // B
    cols_count = FF // B
    column_count = cols_count // N_TENSOR
    subkeys = jax.random.split(key, 8)
    old_cols = jax.random.permutation(subkeys[0], cols_count).astype(jnp.int32).reshape(N_TENSOR, column_count)
    row_order = jax.vmap(lambda subkey: jax.random.permutation(subkey, rows_count))(jax.random.split(subkeys[1], cols_count)).astype(jnp.int32)
    seating = jax.random.permutation(subkeys[2], N_TENSOR).astype(jnp.int32)
    shifts = jax.random.permutation(subkeys[3], N_TENSOR - 1)[:SWAP].astype(jnp.int32) + 1
    by_seat = old_cols[seating]
    staying = by_seat[:, SWAP:]
    senders = jnp.mod(jnp.arange(N_TENSOR, dtype=jnp.int32)[:, None] - shifts[None, :], N_TENSOR)
    incoming = by_seat[senders, jnp.arange(SWAP, dtype=jnp.int32)[None, :]]
    new_by_seat = jnp.concatenate([staying, incoming], axis=1)
    new_cols = jnp.zeros_like(new_by_seat).at[seating].set(new_by_seat)
    pairing = jax.vmap(lambda subkey: jax.random.permutation(subkey, column_count))(jax.random.split(subkeys[4], N_TENSOR)).astype(jnp.int32)
    amount = jax.random.randint(subkeys[5], (N_TENSOR, column_count // 2), -DROP, DROP + 1).astype(jnp.int32)
    shuffled_delta = jnp.concatenate([amount, -amount], axis=1)
    delta = jnp.zeros((N_TENSOR, column_count), jnp.int32).at[jnp.arange(N_TENSOR)[:, None], pairing].set(shuffled_delta)
    growth = DROP + delta
    old_ids = row_order[old_cols][:, :, :KB] * cols_count + old_cols[:, :, None]
    old_list = old_ids.reshape(N_TENSOR, column_count * KB)
    rows_new = row_order[new_cols]
    keep_ids = rows_new[:, :, :KB - DROP]
    grow_ids = rows_new[:, :, KB:KB + 2 * DROP]
    grow_valid = jnp.arange(2 * DROP, dtype=jnp.int32)[None, None, :] < growth[:, :, None]
    candidates = jnp.concatenate([keep_ids, grow_ids], axis=2) * cols_count + new_cols[:, :, None]
    valid = jnp.concatenate([jnp.ones(keep_ids.shape, jnp.int32), grow_valid.astype(jnp.int32)], axis=2)
    candidates = candidates.reshape(N_TENSOR, -1)
    valid = valid.reshape(N_TENSOR, -1)
    ordering = jnp.argsort(1 - valid, axis=1, stable=True)
    new_list = jnp.take_along_axis(candidates, ordering, axis=1)[:, :column_count * KB]
    old_shuffle = jax.vmap(lambda subkey: jax.random.permutation(subkey, column_count * KB))(jax.random.split(subkeys[6], N_TENSOR))
    new_shuffle = jax.vmap(lambda subkey: jax.random.permutation(subkey, column_count * KB))(jax.random.split(subkeys[7], N_TENSOR))
    old_list = jnp.take_along_axis(old_list, old_shuffle, axis=1)
    new_list = jnp.take_along_axis(new_list, new_shuffle, axis=1)
    return (old_list.astype(jnp.int32), new_list.astype(jnp.int32), new_cols.astype(jnp.int32))


def draw_old_blocks(key, part):
    tables = layout(key)
    return tables[0]


def draw_new_blocks(key, part):
    tables = layout(key)
    return tables[1]


def draw_new_columns(key, part):
    tables = layout(key)
    return tables[2]


def shard_levels(key, dims, cuts, low, top_value):
    factor_of, own = 1.0, jax.random.fold_in(key, 6)
    for dim, parts in cuts:
        steps = jnp.exp(jax.random.uniform(jax.random.fold_in(own, dim), (parts,), jnp.float32, low / len(cuts), top_value / len(cuts)))
        factor_of = factor_of * jnp.repeat(steps, dims[dim] // parts).reshape([-1 if axis == dim else 1 for axis in range(len(dims))])
    return factor_of


def noise(own_key, extent, scale, bound, cuts=(), kind=jnp.bfloat16):
    result = scale * jax.random.normal(own_key, extent, jnp.float32)
    if cuts:
        result = result * shard_levels(own_key, extent, cuts, -0.22, 0.18)
    return jnp.clip(result, -bound, bound).astype(kind)


def setup_inputs(seed: int = 0) -> dict:
    streams_of = jax.random.split(jax.random.key(seed), 9)
    return {
        "tokens": noise(streams_of[0], (TOKENS, D), 4.0, 24.0, ((0, 16), (1, 16))),
        "upstream": noise(streams_of[1], (TOKENS, FF), (TOKENS ** -0.5), 0.15625, ((0, 16), (1, 16))),
        "master_weights": noise(streams_of[2], (B, N_TENSOR * CAP, B), 0.005, 0.03, ((0, 16), (1, 16)), jnp.float32),
        "first_moment": noise(streams_of[3], (B, N_TENSOR * CAP, B), 0.1, 0.5, ((0, 16), (1, 16)), jnp.float32),
        "second_moment": jnp.clip(jnp.exp(math.log(0.5) - 2.3025851 * jax.random.uniform(streams_of[4], (B, N_TENSOR * CAP, B), jnp.float32) ** shard_levels(streams_of[4], (B, N_TENSOR * CAP, B), ((0, 16), (1, 16)), -0.2, 0.2)), 0.05, 0.5),
        "old_blocks": draw_old_blocks(jax.random.fold_in(streams_of[8], 71), 0),
        "new_blocks": draw_new_blocks(jax.random.fold_in(streams_of[8], 71), 0),
        "new_columns": draw_new_columns(jax.random.fold_in(streams_of[8], 71), 0),
    }


tanh_scale = 0.7978845608
cubic_coef = 0.044715
beta_one = 0.9
beta_two = 0.95
adam_eps = 1e-08
learn_rate = 0.002
weight_decay = 0.1

def gelu_tanh(values):
    inner = tanh_scale * (values + cubic_coef * values * values * values)
    return 0.5 * values * (1.0 + jnp.tanh(inner))

def gelu_slope(values):
    inner = tanh_scale * (values + cubic_coef * values * values * values)
    tangent = jnp.tanh(inner)
    return 0.5 * (1.0 + tangent) + 0.5 * values * (1.0 - tangent * tangent) * tanh_scale * (1.0 + 3.0 * cubic_coef * values * values)

def adam_update(master, first, second, weight_grad, kept_mask):
    new_first = beta_one * first + (1.0 - beta_one) * weight_grad
    new_second = beta_two * second + (1.0 - beta_two) * weight_grad * weight_grad
    first_hat = new_first / (1.0 - beta_one ** STEP)
    second_hat = new_second / (1.0 - beta_two ** STEP)
    denominator = jnp.where(kept_mask, jnp.sqrt(second_hat) + adam_eps, jnp.float32(1.0))
    new_master = jnp.where(kept_mask, master - learn_rate * (first_hat / denominator + weight_decay * master), jnp.float32(0.0))
    return (new_master, new_first, new_second)

def reference(tokens, upstream, master_weights, first_moment, second_moment, old_blocks, new_blocks, new_columns):
    owners = N_TENSOR
    total = owners * CAP
    old_flat = old_blocks.reshape(-1)
    new_flat = new_blocks.reshape(-1)
    matches = new_flat[:, None] == old_flat[None, :]
    located = jnp.any(matches, axis=1)
    positions = jnp.arange(total, dtype=jnp.int32)
    anchor = lax.optimization_barrier(jnp.sum(jnp.where(matches, positions[None, :], 0), axis=1)).astype(jnp.int32)

    def carry_over(state):
        return jnp.where(located[None, :, None], jnp.take(state, anchor, axis=1), jnp.float32(0.0))
    kept_master = carry_over(master_weights)
    kept_first = carry_over(first_moment)
    kept_second = carry_over(second_moment)
    pieces = tokens.reshape(TOKENS, NBR, B)

    def owner_step(owner_index):
        blocks = lax.dynamic_slice_in_dim(new_blocks, owner_index, 1, 0)[0]
        columns = lax.dynamic_slice_in_dim(new_columns, owner_index, 1, 0)[0]
        master = lax.dynamic_slice_in_dim(kept_master, owner_index * CAP, CAP, 1)
        first = lax.dynamic_slice_in_dim(kept_first, owner_index * CAP, CAP, 1)
        second = lax.dynamic_slice_in_dim(kept_second, owner_index * CAP, CAP, 1)
        kept_mask = lax.dynamic_slice_in_dim(located, owner_index * CAP, CAP, 0)[None, :, None]
        block_row = (blocks // NBC).astype(jnp.int32)
        block_col = (blocks % NBC).astype(jnp.int32)
        placed = block_col[:, None] == columns[None, :]
        place_idx = lax.optimization_barrier(jnp.sum(jnp.where(placed, jnp.arange(CPD, dtype=jnp.int32)[None, :], 0), axis=1)).astype(jnp.int32)
        x_rows = jnp.take(pieces, block_row, axis=1).astype(jnp.float32)
        copy_in = lax.optimization_barrier(master.astype(jnp.bfloat16)).astype(jnp.float32)
        partial_sums = jnp.einsum('tsu,usv->tsv', x_rows, copy_in, precision=lax.Precision.HIGHEST)
        summed = jnp.einsum('tsv,sk->tkv', partial_sums, placed.astype(jnp.float32), precision=lax.Precision.HIGHEST)
        hidden = gelu_tanh(summed).astype(jnp.bfloat16).reshape(TOKENS, CPD * B)
        cotangent = lax.dynamic_slice_in_dim(upstream, owner_index * CPD * B, CPD * B, 1).reshape(TOKENS, CPD, B).astype(jnp.float32)
        local_grad = lax.optimization_barrier((cotangent * gelu_slope(summed)).astype(jnp.bfloat16)).astype(jnp.float32)
        grad_rows = jnp.take(local_grad, place_idx, axis=1)
        weight_grad = jnp.einsum('tsu,tsv->usv', x_rows, grad_rows, precision=lax.Precision.HIGHEST)
        new_master, new_first, new_second = adam_update(master, first, second, weight_grad, kept_mask)
        return (hidden, new_master, new_first, new_second, new_master.astype(jnp.bfloat16))
    results = lax.map(owner_step, jnp.arange(owners, dtype=jnp.int32))
    hidden_out = jnp.transpose(results[0], (1, 0, 2)).reshape(TOKENS, FF)

    def relay(stacked):
        return jnp.transpose(stacked, (1, 0, 2, 3)).reshape(B, total, B)
    return (hidden_out, relay(results[1]), relay(results[2]), relay(results[3]), relay(results[4]))
```

```python
import functools

import jax
import jax.numpy as jnp
from jax import lax
from jax.experimental import pallas as pl
from jax.experimental.pallas import tpu as pltpu
from jax.sharding import PartitionSpec as P

STEP = 20
tanh_scale = 0.7978845608
cubic_coef = 0.044715
beta_one = 0.9
beta_two = 0.95
adam_eps = 1e-08
learn_rate = 0.002
weight_decay = 0.1

OWNERS = 16
SLOTS = 60
KEEP = 3
COLS = 12
B = 128
ROWS = 8
NBC = 192
PER_COL = 8
ZN = 8
F32 = jnp.float32
BF16 = jnp.bfloat16
VMEM_LIMIT = 56 * 1024 * 1024


def vmem():
    return pl.BlockSpec(memory_space=pltpu.VMEM)


def smem():
    return pl.BlockSpec(memory_space=pltpu.SMEM)


SEND, PLACE, BROW, BCOL, LIST = range(5)


def routing_kernel(me_ref, old_ref, new_ref, cols_ref, table_ref):
    me = me_ref[0]
    n = SLOTS
    sub = lax.broadcasted_iota(jnp.int32, (n, n), 0)
    lane = lax.broadcasted_iota(jnp.int32, (n, n), 1)
    eye = sub == lane
    wide = lax.broadcasted_iota(jnp.int32, (n, 128), 1).astype(F32)
    slot = lax.broadcasted_iota(jnp.int32, (n, 128), 0).astype(F32)

    def to_col(row):
        return jnp.sum(jnp.where(eye, row, 0.0), axis=1, keepdims=True)

    def to_row(col):
        return jnp.sum(jnp.where(eye, col, 0.0), axis=0, keepdims=True)

    old_all = old_ref[...].astype(F32)
    new_all = new_ref[...].astype(F32)
    old_row = old_ref[pl.ds(me, 1), :].astype(F32)
    new_row = new_ref[pl.ds(me, 1), :].astype(F32)
    old_col = to_col(old_row)
    new_col = to_col(new_row)
    lane_f = lane.astype(F32)
    me_f = me.astype(F32) + 1.0
    zero = jnp.zeros((n, n), F32)
    target = zero
    source = zero
    source_slot = zero
    for o in range(OWNERS):
        target = target + jnp.where(old_col == new_all[o : o + 1, :], o + 1.0, 0.0)
        hit = new_col == old_all[o : o + 1, :]
        source = source + jnp.where(hit, o + 1.0, 0.0)
        source_slot = source_slot + jnp.where(hit, lane_f, 0.0)
    target = jnp.sum(target, axis=1, keepdims=True)
    source = jnp.sum(source, axis=1, keepdims=True)
    source_slot = jnp.sum(source_slot, axis=1, keepdims=True)

    def rank(kind_col, id_row, id_col):
        same = (to_row(kind_col) == kind_col) & (id_row < id_col)
        return jnp.sum(jnp.where(same, 1.0, 0.0), axis=1, keepdims=True)

    moving = (target > 0.0) & (target != me_f)
    packet = jnp.where(moving, (target - 1.0) * KEEP + rank(target, old_row, old_col), -1.0)
    send = n + jnp.sum(jnp.where(packet == wide, slot - n, 0.0), axis=0, keepdims=True)

    arrived = n + 1.0 + (source - 1.0) * KEEP + rank(source, new_row, new_col)
    place = jnp.where(source == 0.0, float(n), jnp.where(source == me_f, source_slot, arrived))

    block_row = jnp.floor((new_col + 0.5) * (1.0 / NBC))
    block_col = new_col - block_row * NBC
    mine = cols_ref[pl.ds(me, 1), :].astype(F32)
    order = lax.broadcasted_iota(jnp.int32, (n, COLS), 1).astype(F32)
    kth = jnp.sum(jnp.where(block_col == mine, order, 0.0), axis=1, keepdims=True)
    slot_row = lane_f[0:1, :]
    within = rank(kth, slot_row, slot[:, 0:1])
    listed = n + jnp.sum(
        jnp.where(kth * PER_COL + within == wide, slot - n, 0.0), axis=0, keepdims=True
    )

    def spread(col):
        return jnp.sum(jnp.where(slot == wide, col, 0.0), axis=0, keepdims=True)

    rows = [send, spread(place), spread(block_row), spread(kth), listed]
    for i, row in enumerate(rows):
        table_ref[i : i + 1, :] = row.astype(jnp.int32)
    table_ref[len(rows) : 8, :] = jnp.zeros((8 - len(rows), 128), jnp.int32)


def pack_kernel(table_ref, master_ref, first_ref, second_ref, held_ref, out_ref):
    for state, ref in enumerate((master_ref, first_ref, second_ref)):
        for u in range(ROWS):
            held_ref[pl.ds(state * ROWS + u, SLOTS, stride=3 * ROWS), :] = ref[u]
    held_ref[SLOTS * 24 : SLOTS * 24 + 24, :] = jnp.zeros((24, 128), F32)

    def step(q, carry):
        at = pl.multiple_of(table_ref[SEND, q] * 24, 8)
        out_ref[pl.ds(pl.multiple_of(q * 24, 8), 24), :] = held_ref[pl.ds(at, 24), :]
        return carry

    lax.fori_loop(0, OWNERS * KEEP, step, 0, unroll=8)


def place_kernel(table_ref, held_ref, arrived_ref, master_ref, first_ref, second_ref, mask_ref, copy_ref):
    def step(s, carry):
        index = table_ref[PLACE, s]
        here = pl.multiple_of(jnp.minimum(index, SLOTS) * 24, 8)
        there = pl.multiple_of(jnp.maximum(index - SLOTS - 1, 0) * 24, 8)
        local_tile = held_ref[pl.ds(here, 24), :]
        moved_tile = arrived_ref[pl.ds(there, 24), :]
        pick = (jnp.zeros((24, 128), jnp.int32) + index) <= SLOTS
        tile = jnp.where(pick, local_tile, moved_tile)
        at = pl.ds(pl.multiple_of(s * 8, 8), 8)
        master_ref[at, :] = tile[0:8]
        first_ref[at, :] = tile[8:16]
        second_ref[at, :] = tile[16:24]
        kept = (jnp.zeros((8, 128), jnp.int32) + index) != SLOTS
        mask_ref[at, :] = jnp.where(kept, 1.0, 0.0)
        return carry

    lax.fori_loop(0, SLOTS, step, 0, unroll=4)
    copy_ref[...] = master_ref[...].astype(BF16)


def main_kernel(*refs):
    table_ref, where_ref, tokens_ref, upstream_ref = refs[:4]
    pieces = refs[4:20]
    hidden_ref = refs[20]
    keep_refs = refs[21:29]
    send_refs = refs[29:37]
    weights, local_grad, grads = refs[37:]
    z = where_ref[0]
    xh = where_ref[1]
    for index, piece in enumerate(pieces):
        rel, other = divmod(index, 2)
        source = lax.rem(z + rel, ZN) * 2 + (lax.rem(xh + other, 2))
        at = pl.ds(pl.multiple_of(source * ROWS, ROWS), ROWS)
        weights[0:SLOTS, at, :] = piece[...].astype(F32).reshape(SLOTS, ROWS, B)
    weights[SLOTS] = jnp.zeros((B, B), F32)

    def block(row):
        lanes = pl.ds(pl.multiple_of(lax.rem(row, 3) * B, B), B)
        return tokens_ref[row // 3, :, lanes]

    def forward(k, carry):
        total = None
        for p in range(PER_COL // 2):
            s0 = table_ref[LIST, k * PER_COL + 2 * p]
            s1 = table_ref[LIST, k * PER_COL + 2 * p + 1]
            x = jnp.concatenate([block(table_ref[BROW, s0]), block(table_ref[BROW, s1])], axis=1)
            w = jnp.concatenate([weights[s0], weights[s1]], axis=0).astype(BF16)
            part = jnp.dot(x, w, preferred_element_type=F32)
            total = part if total is None else total + part
        lanes = pl.ds(pl.multiple_of(k * B, B), B)
        square = total * total
        tangent = jnp.tanh(tanh_scale * (total + cubic_coef * square * total))
        half = 0.5 * (1.0 + tangent)
        hidden_ref[:, lanes] = (total * half).astype(BF16)
        slope = half + 0.5 * total * (1.0 - tangent * tangent) * tanh_scale * (
            1.0 + 3.0 * cubic_coef * square
        )
        local_grad[k] = (upstream_ref[:, lanes].astype(F32) * slope).astype(BF16)
        return carry

    lax.fori_loop(0, COLS, forward, 0)

    def backward(p, carry):
        for half in range(2):
            s = 2 * p + half
            x = block(table_ref[BROW, s])
            g = local_grad[table_ref[BCOL, s]]
            grads[half * B : (half + 1) * B, :] = lax.dot_general(
                x, g, (((0,), (0,)), ((), ())), preferred_element_type=F32
            )
        at = pl.ds(pl.multiple_of(p * 16, 16), 16)
        for rel in range(ZN):
            base = lax.rem(z + rel, ZN) * 16
            mine = base + xh * ROWS
            other = base + (1 - xh) * ROWS

            def pair(start):
                a = grads[pl.ds(pl.multiple_of(start, ROWS), ROWS), :]
                b = grads[pl.ds(pl.multiple_of(start + B, ROWS), ROWS), :]
                return jnp.concatenate([a, b], axis=0)

            keep_refs[rel][at, :] = pair(mine)
            send_refs[rel][at, :] = pair(other).astype(BF16)
        return carry

    lax.fori_loop(0, SLOTS // 2, backward, 0)


def adam_kernel(
    own_ref, got_ref, up_ref, down_ref, mast_ref, mom_ref, var_ref, mask_ref,
    master_ref, first_ref, second_ref, copy_ref, out_m, out_f, out_s,
):
    grad = own_ref[...] + got_ref[...].astype(F32) + up_ref[...].astype(F32) + down_ref[...].astype(F32)
    master = mast_ref[...]
    kept = mask_ref[...] > 0.5
    new_first = beta_one * mom_ref[...] + (1.0 - beta_one) * grad
    new_second = beta_two * var_ref[...] + (1.0 - beta_two) * grad * grad
    first_hat = new_first / (1.0 - beta_one**STEP)
    second_hat = new_second / (1.0 - beta_two**STEP)
    denominator = jnp.where(kept, jnp.sqrt(second_hat) + adam_eps, 1.0)
    out_m[...] = jnp.where(
        kept, master - learn_rate * (first_hat / denominator + weight_decay * master), 0.0
    )
    out_f[...] = new_first
    out_s[...] = new_second
    for u in range(ROWS):
        at = pl.ds(u, SLOTS, stride=ROWS)
        new_master = out_m[at, :]
        master_ref[u] = new_master
        copy_ref[u] = new_master.astype(BF16)
        first_ref[u] = out_f[at, :]
        second_ref[u] = out_s[at, :]


SWAP = [(i, i ^ 1) for i in range(16)]
UP = [(i, (i + 2) % 16) for i in range(16)]
DOWN = [(i, (i - 2) % 16) for i in range(16)]


def gather_pieces(shard):
    pieces = [[None, None] for _ in range(ZN)]
    swapped = lax.ppermute(shard, "dp", SWAP)
    up = [shard, swapped]
    down = [shard, swapped]
    pieces[0] = [shard, swapped]
    for step in range(1, 4):
        for j in range(2):
            up[j] = lax.ppermute(up[j], "dp", UP)
            down[j] = lax.ppermute(down[j], "dp", DOWN)
            pieces[ZN - step][j] = up[j]
            pieces[step][j] = down[j]
    pieces[4][0] = lax.ppermute(up[0], "dp", UP)
    pieces[4][1] = lax.ppermute(down[1], "dp", DOWN)
    return pieces


def local(tokens, upstream, master_weights, first_moment, second_moment, old_blocks, new_blocks, new_columns):
    owner = lax.axis_index("tensor")
    dp = lax.axis_index("dp")
    z = dp // 2
    xh = dp % 2
    me = jnp.reshape(owner, (1,)).astype(jnp.int32)
    where = jnp.stack([z, xh]).astype(jnp.int32)
    params = pltpu.CompilerParams(vmem_limit_bytes=VMEM_LIMIT)
    shape = jax.ShapeDtypeStruct

    gathered = lax.all_gather(tokens, "tensor", axis=0)

    table = pl.pallas_call(
        routing_kernel,
        out_shape=shape((8, 128), jnp.int32),
        in_specs=[smem(), vmem(), vmem(), vmem()],
        out_specs=vmem(),
        compiler_params=params,
    )(me, old_blocks, new_blocks, new_columns)

    held, packed = pl.pallas_call(
        pack_kernel,
        out_shape=(shape(((SLOTS + 1) * 24, 128), F32), shape((OWNERS * KEEP * 24, 128), F32)),
        in_specs=[smem()] + [vmem()] * 3,
        out_specs=(vmem(),) * 2,
        compiler_params=params,
    )(table, master_weights, first_moment, second_moment)
    arrived = lax.all_to_all(packed, "tensor", split_axis=0, concat_axis=0, tiled=True)

    flat = shape((SLOTS * ROWS, 128), F32)
    flat16 = shape((SLOTS * ROWS, 128), BF16)
    kept_master, kept_first, kept_second, mask, copy_in = pl.pallas_call(
        place_kernel,
        out_shape=(flat, flat, flat, flat, flat16),
        in_specs=[smem()] + [vmem()] * 2,
        out_specs=(vmem(),) * 5,
        compiler_params=params,
    )(table, held, arrived)

    pieces = gather_pieces(copy_in)
    flat_pieces = [piece for pair in pieces for piece in pair]

    tokens_here = tokens.shape[0]
    results = pl.pallas_call(
        main_kernel,
        out_shape=(shape((tokens_here, COLS * B), BF16),) + (flat,) * ZN + (flat16,) * ZN,
        in_specs=[smem()] * 2 + [vmem()] * 18,
        out_specs=(vmem(),) * 17,
        scratch_shapes=[
            pltpu.VMEM((SLOTS + 1, B, B), F32),
            pltpu.VMEM((COLS, tokens_here, B), BF16),
            pltpu.VMEM((2 * B, B), F32),
        ],
        compiler_params=params,
        cost_estimate=pl.CostEstimate(flops=4 * 10**9, bytes_accessed=2 * 10**7, transcendentals=10**6),
    )(table, where, gathered, upstream, *flat_pieces)
    hidden_out = results[0]
    keep = results[1:9]
    send = results[9:17]

    got = [None] * ZN
    for rel in (4, 3, 5, 2, 6, 1, 7, 0):
        got[rel] = lax.ppermute(send[rel], "dp", SWAP)

    def joined(rel):
        return keep[rel] + got[rel].astype(F32)

    half = SLOTS * ROWS // 2
    far = joined(4)
    up = lax.ppermute(far[:half].astype(BF16), "dp", UP)
    down = lax.ppermute(far[half:].astype(BF16), "dp", DOWN)
    zeros = jnp.zeros((half, 128), F32)
    up = jnp.concatenate([up.astype(F32), zeros], axis=0)
    down = jnp.concatenate([zeros, down.astype(F32)], axis=0)
    for step in (3, 2, 1):
        up = lax.ppermute((joined(step) + up.astype(F32)).astype(BF16), "dp", UP)
        down = lax.ppermute((joined(ZN - step) + down.astype(F32)).astype(BF16), "dp", DOWN)

    state = shape((ROWS, SLOTS, B), F32)
    new_master, new_first, new_second, fresh = pl.pallas_call(
        adam_kernel,
        out_shape=(state, state, state, shape((ROWS, SLOTS, B), BF16)),
        in_specs=[vmem()] * 8,
        out_specs=(vmem(),) * 4,
        scratch_shapes=[pltpu.VMEM((SLOTS * ROWS, 128), F32)] * 3,
        compiler_params=params,
    )(keep[0], got[0], up, down, kept_master, kept_first, kept_second, mask)

    final = gather_pieces(fresh)
    weight_copy = jnp.zeros((16, ROWS, SLOTS, B), BF16)
    for rel in (0, 1, 7, 2, 6, 3, 5, 4):
        for j in range(2):
            source = lax.rem(z + rel, ZN) * 2 + lax.rem(xh + j, 2)
            weight_copy = lax.dynamic_update_slice(weight_copy, final[rel][j][None], (source, 0, 0, 0))
    weight_copy = weight_copy.reshape(16 * ROWS, SLOTS, B)
    return (hidden_out, new_master, new_first, new_second, weight_copy)


def solution(mesh):
    split = P("dp", "tensor", None)
    return jax.shard_map(
        local,
        mesh=mesh,
        in_specs=(P("dp", "tensor"), P("dp", "tensor"), split, split, split, P(), P(), P()),
        out_specs=(P("dp", "tensor"), split, split, split, P(None, "tensor", None)),
        check_vma=False,
    )
```

```python
import itertools

import jax
import jax.numpy as jnp
from jax import lax
from jax.experimental import pallas as pl
from jax.experimental.pallas import tpu as pltpu
from jax.sharding import PartitionSpec as P

STEP = 20
tanh_scale = 0.7978845608
cubic_coef = 0.044715
beta_one = 0.9
beta_two = 0.95
adam_eps = 1e-08
learn_rate = 0.002
weight_decay = 0.1

OWNERS = 16
SLOTS = 60
KEEP = 3
COLS = 12
KEPT = COLS * KEEP
B = 128
ROWS = 8
NBC = 192
ZN = 8
F32 = jnp.float32
BF16 = jnp.bfloat16
PARAMS = pltpu.CompilerParams(vmem_limit_bytes=56 * 1024 * 1024)

SEND, PLACE, BROW, BCOL, LIST, RANK = range(6)


def vmem():
    return pl.BlockSpec(memory_space=pltpu.VMEM)


def smem():
    return pl.BlockSpec(memory_space=pltpu.SMEM)


def sd(shape, dtype):
    return jax.ShapeDtypeStruct(shape, dtype)


def routing_table(me, old_ref, new_ref, cols_ref):
    n = SLOTS
    sub = lax.broadcasted_iota(jnp.int32, (n, n), 0)
    lane = lax.broadcasted_iota(jnp.int32, (n, n), 1)
    eye = sub == lane
    wide = lax.broadcasted_iota(jnp.int32, (n, 128), 1).astype(F32)
    slot = lax.broadcasted_iota(jnp.int32, (n, 128), 0).astype(F32)

    def to_col(row):
        return jnp.sum(jnp.where(eye, row, 0.0), axis=1, keepdims=True)

    def to_row(col):
        return jnp.sum(jnp.where(eye, col, 0.0), axis=0, keepdims=True)

    old_all = old_ref[...].astype(F32)
    new_all = new_ref[...].astype(F32)
    old_row = old_ref[pl.ds(me, 1), :].astype(F32)
    new_row = new_ref[pl.ds(me, 1), :].astype(F32)
    old_col = to_col(old_row)
    new_col = to_col(new_row)
    lane_f = lane.astype(F32)
    me_f = me.astype(F32) + 1.0
    zero = jnp.zeros((n, n), F32)
    target = zero
    source = zero
    source_slot = zero
    for o in range(OWNERS):
        target = target + jnp.where(old_col == new_all[o : o + 1, :], o + 1.0, 0.0)
        hit = new_col == old_all[o : o + 1, :]
        source = source + jnp.where(hit, o + 1.0, 0.0)
        source_slot = source_slot + jnp.where(hit, lane_f, 0.0)
    target = jnp.sum(target, axis=1, keepdims=True)
    source = jnp.sum(source, axis=1, keepdims=True)
    source_slot = jnp.sum(source_slot, axis=1, keepdims=True)

    def rank(kind_col, id_row, id_col):
        same = (to_row(kind_col) == kind_col) & (id_row < id_col)
        return jnp.sum(jnp.where(same, 1.0, 0.0), axis=1, keepdims=True)

    def listing(entry_col):
        return n + jnp.sum(jnp.where(entry_col == wide, slot - n, 0.0), axis=0, keepdims=True)

    moving = (target > 0.0) & (target != me_f)
    packet = jnp.where(moving, (target - 1.0) * KEEP + rank(target, old_row, old_col), -1.0)

    arrived = n + 1.0 + (source - 1.0) * KEEP + rank(source, new_row, new_col)
    kept = source > 0.0
    place = jnp.where(kept, jnp.where(source == me_f, source_slot, arrived), float(n))

    block_row = jnp.floor((new_col + 0.5) * (1.0 / NBC))
    block_col = new_col - block_row * NBC
    mine = cols_ref[pl.ds(me, 1), :].astype(F32)
    order = lax.broadcasted_iota(jnp.int32, (n, COLS), 1).astype(F32)
    kth = jnp.sum(jnp.where(block_col == mine, order, 0.0), axis=1, keepdims=True)
    kept_kth = jnp.where(kept, kth, -1.0)
    within = rank(kept_kth, lane_f[0:1, :], slot[:, 0:1])
    entry = jnp.where(kept, kth * KEEP + within, float(KEPT))

    def spread(col):
        return jnp.sum(jnp.where(slot == wide, col, 0.0), axis=0, keepdims=True)

    return [
        listing(packet), spread(place), spread(block_row), spread(kth), listing(entry), spread(entry),
    ]


def pack_kernel(
    me_ref, old_ref, new_ref, cols_ref, master_ref, first_ref, second_ref, table_ref, out_ref, scalars, sem
):
    rows = routing_table(me_ref[0], old_ref, new_ref, cols_ref)
    for i, row in enumerate(rows):
        table_ref[i : i + 1, :] = row.astype(jnp.int32)
    table_ref[len(rows) : 8, :] = jnp.zeros((8 - len(rows), 128), jnp.int32)
    copy = pltpu.make_async_copy(table_ref, scalars, sem)
    copy.start()
    copy.wait()

    def step(q, carry):
        slot = scalars[SEND, q]
        at = jnp.minimum(slot, SLOTS - 1)
        some = (jnp.zeros((ROWS, B), jnp.int32) + slot) < SLOTS
        for state, ref in enumerate((master_ref, first_ref, second_ref)):
            out_ref[q, state] = jnp.where(some, ref[at], 0.0)
        return carry

    lax.fori_loop(0, OWNERS * KEEP, step, 0, unroll=8)


def place_kernel(
    table_ref, master_in, first_in, second_in, arrived_ref,
    copy_ref, master_ref, first_ref, second_ref, mask_ref, scratch,
):
    def step(s, carry):
        index = table_ref[PLACE, s]
        here = jnp.minimum(index, SLOTS - 1)
        there = jnp.maximum(index - SLOTS - 1, 0)
        tag = jnp.zeros((ROWS, B), jnp.int32) + index
        kept = tag != SLOTS
        at = pl.ds(pl.multiple_of(s * ROWS, ROWS), ROWS)
        for state, (ref, out) in enumerate(
            ((master_in, master_ref), (first_in, first_ref), (second_in, second_ref))
        ):
            tile = jnp.where(tag < SLOTS, ref[here], arrived_ref[there, state])
            out[at, :] = jnp.where(kept, tile, 0.0)
        mask_ref[at, :] = jnp.where(kept, 1.0, 0.0)
        return carry

    lax.fori_loop(0, SLOTS, step, 0, unroll=6)

    def pick(i, carry):
        at = pl.ds(pl.multiple_of(table_ref[LIST, i] * ROWS, ROWS), ROWS)
        scratch[pl.ds(pl.multiple_of(i * ROWS, ROWS), ROWS), :] = master_ref[at, :]
        return carry

    lax.fori_loop(0, KEPT, pick, 0, unroll=6)
    copy_ref[...] = scratch[...].astype(BF16)


def assemble(pieces, z, xh, weights):
    for index, piece in enumerate(pieces):
        rel, other = divmod(index, 2)
        source = lax.rem(z + rel, ZN) * 2 + lax.rem(xh + other, 2)
        at = pl.ds(pl.multiple_of(source * ROWS, ROWS), ROWS)
        weights[:, at, :] = piece[...].astype(F32).reshape(KEPT, ROWS, B)


def main_kernel(*refs):
    table_ref, where_ref, tokens_ref, upstream_ref = refs[:4]
    pieces = refs[4:20]
    hidden_ref, keep_ref, send_ref = refs[20:23]
    weights, local_grad, grads = refs[23:]
    z = where_ref[0]
    xh = where_ref[1]
    sign = where_ref[2]
    assemble(pieces, z, xh, weights)

    def block(row):
        lanes = pl.ds(pl.multiple_of(lax.rem(row, 3) * B, B), B)
        return tokens_ref[row // 3, :, lanes]

    def forward(k, carry):
        xs = [block(table_ref[BROW, table_ref[LIST, k * KEEP + j]]) for j in range(KEEP)]
        w = jnp.concatenate([weights[k * KEEP + j] for j in range(KEEP)], axis=0).astype(BF16)
        total = jnp.dot(jnp.concatenate(xs, axis=1), w, preferred_element_type=F32)
        lanes = pl.ds(pl.multiple_of(k * B, B), B)
        square = total * total
        tangent = jnp.tanh(tanh_scale * (total + cubic_coef * square * total))
        half = 0.5 * (1.0 + tangent)
        hidden_ref[:, lanes] = (total * half).astype(BF16)
        slope = half + 0.5 * total * (1.0 - tangent * tangent) * tanh_scale * (
            1.0 + 3.0 * cubic_coef * square
        )
        local_grad[k] = (upstream_ref[:, lanes].astype(F32) * slope).astype(BF16)
        return carry

    lax.fori_loop(0, COLS, forward, 0)

    def backward(p, carry):
        for half in range(2):
            s = 2 * p + half
            x = block(table_ref[BROW, s])
            g = local_grad[table_ref[BCOL, s]]
            grads[half * B : (half + 1) * B, :] = lax.dot_general(
                x, g, (((0,), (0,)), ((), ())), preferred_element_type=F32
            )
        at = pl.ds(pl.multiple_of(p * 16, 16), 16)
        for rel in range(ZN):
            base = lax.rem(z + sign * rel + ZN, ZN) * 16

            def pair(start):
                a = grads[pl.ds(pl.multiple_of(start, ROWS), ROWS), :]
                b = grads[pl.ds(pl.multiple_of(start + B, ROWS), ROWS), :]
                return jnp.concatenate([a, b], axis=0)

            keep_ref[rel, at, :] = pair(base + xh * ROWS)
            send_ref[rel, at, :] = pair(base + (1 - xh) * ROWS).astype(BF16)
        return carry

    lax.fori_loop(0, SLOTS // 2, backward, 0)


def adam_kernel(
    table_ref, own_ref, got_ref, near_ref, last_ref, mast_ref, mom_ref, var_ref, mask_ref,
    master_ref, first_ref, second_ref, copy_ref, scratch,
):
    grad = own_ref[...] + got_ref[...].astype(F32)
    grad = grad + near_ref[...].astype(F32) + last_ref[...].astype(F32)
    master = mast_ref[...]
    kept = mask_ref[...] > 0.5
    new_first = beta_one * mom_ref[...] + (1.0 - beta_one) * grad
    new_second = beta_two * var_ref[...] + (1.0 - beta_two) * grad * grad
    first_hat = new_first / (1.0 - beta_one**STEP)
    second_hat = new_second / (1.0 - beta_two**STEP)
    denominator = jnp.where(kept, jnp.sqrt(second_hat) + adam_eps, 1.0)
    master_ref[...] = jnp.where(
        kept, master - learn_rate * (first_hat / denominator + weight_decay * master), 0.0
    )
    first_ref[...] = new_first
    second_ref[...] = new_second

    def pick(i, carry):
        at = pl.ds(pl.multiple_of(table_ref[LIST, i] * ROWS, ROWS), ROWS)
        scratch[pl.ds(pl.multiple_of(i * ROWS, ROWS), ROWS), :] = master_ref[at, :]
        return carry

    lax.fori_loop(0, KEPT, pick, 0, unroll=6)
    copy_ref[...] = scratch[...].astype(BF16)


def final_kernel(*refs):
    table_ref, where_ref = refs[:2]
    pieces = refs[2:18]
    out_ref, weights = refs[18:]
    assemble(pieces, where_ref[0], where_ref[1], weights)

    def step(s, carry):
        entry = table_ref[RANK, s]
        some = (jnp.zeros((B, B), jnp.int32) + entry) < KEPT
        out_ref[s] = jnp.where(some, weights[jnp.minimum(entry, KEPT - 1)], 0.0).astype(BF16)
        return carry

    lax.fori_loop(0, SLOTS, step, 0, unroll=2)


AXES = ("dp", "tensor")
SWAP = [(i, i ^ 1) for i in range(16)]
UP = [(i, (i + 2) % 16) for i in range(16)]
DOWN = [(i, (i - 2) % 16) for i in range(16)]


def direction(z, core):
    return 1 - 2 * ((z + core) % 2)


def exchange(side):
    out = []
    for z, xh, t in itertools.product(range(ZN), range(2), range(16)):
        other = (z + side * direction(z, t % 2)) % ZN
        out.append(((z * 2 + xh) * 16 + t, (other * 2 + xh) * 16 + t))
    return out


NEAR = exchange(1)
FAR = exchange(-1)


def gather_pieces(shard):
    pieces = [[None, None] for _ in range(ZN)]
    swapped = lax.ppermute(shard, "dp", SWAP)
    up = [shard, swapped]
    down = [shard, swapped]
    pieces[0] = [shard, swapped]
    for step in range(1, 4):
        for j in range(2):
            up[j] = lax.ppermute(up[j], "dp", UP)
            down[j] = lax.ppermute(down[j], "dp", DOWN)
            pieces[ZN - step][j] = up[j]
            pieces[step][j] = down[j]
    pieces[4][0] = lax.ppermute(up[0], "dp", UP)
    pieces[4][1] = lax.ppermute(down[1], "dp", DOWN)
    return [piece for pair in pieces for piece in pair]


def reduce_chunks(keep, send):
    joined = {}
    for group in ((4, 5), (2, 3), (6, 7), (0, 1)):
        got = lax.ppermute(send[group[0] : group[1] + 1], "dp", SWAP)
        for i, rel in enumerate(group):
            joined[rel] = (keep[rel], got[i])

    def total(rel, more=None):
        value = joined[rel][0] + joined[rel][1].astype(F32)
        return (value if more is None else value + more.astype(F32)).astype(BF16)

    a = lax.ppermute(jnp.stack([total(5), total(4)]), AXES, FAR)
    b = lax.ppermute(jnp.stack([total(2, a[0]), total(3, a[1])]), AXES, NEAR)
    c = lax.ppermute(jnp.stack([total(7, b[0]), total(6, b[1])]), AXES, FAR)
    d = lax.ppermute(total(1, c[1]), AXES, NEAR)
    return joined[0][0], joined[0][1], c[0], d


def local(tokens, upstream, master_weights, first_moment, second_moment, old_blocks, new_blocks, new_columns):
    owner = lax.axis_index("tensor")
    dp = lax.axis_index("dp")
    z = dp // 2
    me = jnp.reshape(owner, (1,)).astype(jnp.int32)
    where = jnp.stack([z, dp % 2, direction(z, owner % 2)]).astype(jnp.int32)
    states = [jnp.transpose(a, (1, 0, 2)) for a in (master_weights, first_moment, second_moment)]

    gathered = lax.all_gather(tokens, "tensor", axis=0)

    table, packed = pl.pallas_call(
        pack_kernel,
        out_shape=(sd((8, 128), jnp.int32), sd((OWNERS * KEEP, 3, ROWS, B), F32)),
        in_specs=[smem()] + [vmem()] * 6,
        out_specs=(vmem(),) * 2,
        scratch_shapes=[pltpu.SMEM((8, 128), jnp.int32), pltpu.SemaphoreType.DMA],
        compiler_params=PARAMS,
    )(me, old_blocks, new_blocks, new_columns, *states)
    arrived = lax.all_to_all(packed, "tensor", split_axis=0, concat_axis=0, tiled=True)

    flat = sd((SLOTS * ROWS, B), F32)
    flat16 = sd((KEPT * ROWS, B), BF16)
    copy_in, kept_master, kept_first, kept_second, mask = pl.pallas_call(
        place_kernel,
        out_shape=(flat16, flat, flat, flat, flat),
        in_specs=[smem()] + [vmem()] * 4,
        out_specs=(vmem(),) * 5,
        scratch_shapes=[pltpu.VMEM((KEPT * ROWS, B), F32)],
        compiler_params=PARAMS,
    )(table, *states, arrived)

    pieces = gather_pieces(copy_in)

    tokens_here = tokens.shape[0]
    hidden_out, keep, send = pl.pallas_call(
        main_kernel,
        out_shape=(
            sd((tokens_here, COLS * B), BF16),
            sd((ZN, SLOTS * ROWS, B), F32),
            sd((ZN, SLOTS * ROWS, B), BF16),
        ),
        in_specs=[smem()] * 2 + [vmem()] * 18,
        out_specs=(vmem(),) * 3,
        scratch_shapes=[
            pltpu.VMEM((KEPT, B, B), F32),
            pltpu.VMEM((COLS, tokens_here, B), BF16),
            pltpu.VMEM((2 * B, B), F32),
        ],
        compiler_params=PARAMS,
        cost_estimate=pl.CostEstimate(flops=4 * 10**9, bytes_accessed=2 * 10**7, transcendentals=10**6),
    )(table, where, gathered, upstream, *pieces)

    grads = reduce_chunks(keep, send)

    new_master, new_first, new_second, fresh = pl.pallas_call(
        adam_kernel,
        out_shape=(flat, flat, flat, flat16),
        in_specs=[smem()] + [vmem()] * 8,
        out_specs=(vmem(),) * 4,
        scratch_shapes=[pltpu.VMEM((KEPT * ROWS, B), F32)],
        compiler_params=PARAMS,
    )(table, *grads, kept_master, kept_first, kept_second, mask)

    final = gather_pieces(fresh)
    weight_copy = pl.pallas_call(
        final_kernel,
        out_shape=sd((SLOTS, B, B), BF16),
        in_specs=[smem()] * 2 + [vmem()] * 16,
        out_specs=vmem(),
        scratch_shapes=[pltpu.VMEM((KEPT, B, B), F32)],
        compiler_params=PARAMS,
    )(table, where, *final)

    def back(a):
        return jnp.transpose(a.reshape(SLOTS, -1, B), (1, 0, 2))

    return (hidden_out, back(new_master), back(new_first), back(new_second), back(weight_copy))


def solution(mesh):
    split = P("dp", "tensor", None)
    return jax.shard_map(
        local,
        mesh=mesh,
        in_specs=(P("dp", "tensor"), P("dp", "tensor"), split, split, split, P(), P(), P()),
        out_specs=(P("dp", "tensor"), split, split, split, P(None, "tensor", None)),
        check_vma=False,
    )
```

```python
import itertools

import jax
import jax.numpy as jnp
from jax import lax
from jax.experimental import pallas as pl
from jax.experimental.pallas import tpu as pltpu
from jax.sharding import PartitionSpec as P

STEP = 20
tanh_scale = 0.7978845608
cubic_coef = 0.044715
beta_one = 0.9
beta_two = 0.95
adam_eps = 1e-08
learn_rate = 0.002
weight_decay = 0.1

OWNERS = 16
SLOTS = 60
KEEP = 3
COLS = 12
KEPT = COLS * KEEP
B = 128
ROWS = 8
NBC = 192
ZN = 8
F32 = jnp.float32
BF16 = jnp.bfloat16


def params(mib):
    return pltpu.CompilerParams(vmem_limit_bytes=mib * 1024 * 1024)

Y_ORDER = ((0,), (1,), (-1, -2))

ORDER = (5, 4, 2, 3, 7, 6, 0, 1)

SEND, PLACE, BROW, BCOL, LIST, RANK = range(6)


def vmem():
    return pl.BlockSpec(memory_space=pltpu.VMEM)


def hbm():
    return pl.BlockSpec(memory_space=pltpu.HBM)


def smem():
    return pl.BlockSpec(memory_space=pltpu.SMEM)


def sd(shape, dtype):
    return jax.ShapeDtypeStruct(shape, dtype)


def routing_table(me, old_ref, new_ref, cols_ref):
    n = SLOTS
    sub = lax.broadcasted_iota(jnp.int32, (n, n), 0)
    lane = lax.broadcasted_iota(jnp.int32, (n, n), 1)
    eye = sub == lane
    wide = lax.broadcasted_iota(jnp.int32, (n, 128), 1).astype(F32)
    slot = lax.broadcasted_iota(jnp.int32, (n, 128), 0).astype(F32)

    def to_col(row):
        return jnp.sum(jnp.where(eye, row, 0.0), axis=1, keepdims=True)

    def to_row(col):
        return jnp.sum(jnp.where(eye, col, 0.0), axis=0, keepdims=True)

    old_all = old_ref[...].astype(F32)
    new_all = new_ref[...].astype(F32)
    old_row = old_ref[pl.ds(me, 1), :].astype(F32)
    new_row = new_ref[pl.ds(me, 1), :].astype(F32)
    old_col = to_col(old_row)
    new_col = to_col(new_row)
    lane_f = lane.astype(F32)
    me_f = me.astype(F32) + 1.0
    zero = jnp.zeros((n, n), F32)
    target = zero
    source = zero
    source_slot = zero
    for o in range(OWNERS):
        target = target + jnp.where(old_col == new_all[o : o + 1, :], o + 1.0, 0.0)
        hit = new_col == old_all[o : o + 1, :]
        source = source + jnp.where(hit, o + 1.0, 0.0)
        source_slot = source_slot + jnp.where(hit, lane_f, 0.0)
    target = jnp.sum(target, axis=1, keepdims=True)
    source = jnp.sum(source, axis=1, keepdims=True)
    source_slot = jnp.sum(source_slot, axis=1, keepdims=True)

    def rank(kind_col, id_row, id_col):
        same = (to_row(kind_col) == kind_col) & (id_row < id_col)
        return jnp.sum(jnp.where(same, 1.0, 0.0), axis=1, keepdims=True)

    def listing(entry_col):
        return n + jnp.sum(jnp.where(entry_col == wide, slot - n, 0.0), axis=0, keepdims=True)

    moving = (target > 0.0) & (target != me_f)
    packet = jnp.where(moving, (target - 1.0) * KEEP + rank(target, old_row, old_col), -1.0)

    arrived = n + 1.0 + (source - 1.0) * KEEP + rank(source, new_row, new_col)
    kept = source > 0.0
    place = jnp.where(kept, jnp.where(source == me_f, source_slot, arrived), float(n))

    block_row = jnp.floor((new_col + 0.5) * (1.0 / NBC))
    block_col = new_col - block_row * NBC
    mine = cols_ref[pl.ds(me, 1), :].astype(F32)
    order = lax.broadcasted_iota(jnp.int32, (n, COLS), 1).astype(F32)
    kth = jnp.sum(jnp.where(block_col == mine, order, 0.0), axis=1, keepdims=True)
    kept_kth = jnp.where(kept, kth, -1.0)
    within = rank(kept_kth, lane_f[0:1, :], slot[:, 0:1])
    entry = jnp.where(kept, kth * KEEP + within, float(KEPT))

    def spread(col):
        return jnp.sum(jnp.where(slot == wide, col, 0.0), axis=0, keepdims=True)

    return [
        listing(packet), spread(place), spread(block_row), spread(kth), listing(entry), spread(entry),
    ]


def pack_kernel(
    me_ref, old_ref, new_ref, cols_ref, master_ref, first_ref, second_ref, table_ref, out_ref, moments_ref, scalars, sem
):
    rows = routing_table(me_ref[0], old_ref, new_ref, cols_ref)
    for i, row in enumerate(rows):
        table_ref[i : i + 1, :] = row.astype(jnp.int32)
    table_ref[len(rows) : 8, :] = jnp.zeros((8 - len(rows), 128), jnp.int32)
    copy = pltpu.make_async_copy(table_ref, scalars, sem)
    copy.start()
    copy.wait()

    def step(q, carry):
        slot = scalars[SEND, q]
        at = jnp.minimum(slot, SLOTS - 1)
        some = (jnp.zeros((ROWS, B), jnp.int32) + slot) < SLOTS
        out_ref[q] = jnp.where(some, master_ref[at], 0.0)
        for state, ref in enumerate((first_ref, second_ref)):
            moments_ref[q, state] = jnp.where(some, ref[at], 0.0)
        return carry

    lax.fori_loop(0, OWNERS * KEEP, step, 0, unroll=8)


def place_tile(table_ref, slot, ref, arrived):
    index = table_ref[PLACE, slot]
    tag = jnp.zeros((ROWS, B), jnp.int32) + index
    here = ref[jnp.minimum(index, SLOTS - 1)]
    there = arrived(jnp.maximum(index - SLOTS - 1, 0))
    return jnp.where(tag < SLOTS, here, there), tag != SLOTS


def copy_in_kernel(table_ref, master_in, arrived_ref, copy_ref, scratch):
    def step(i, carry):
        tile, _ = place_tile(table_ref, table_ref[LIST, i], master_in, lambda at: arrived_ref[at])
        scratch[pl.ds(pl.multiple_of(i * ROWS, ROWS), ROWS), :] = tile
        return carry

    lax.fori_loop(0, KEPT, step, 0, unroll=12)
    for i in range(2 * ZN):
        copy_ref[i] = scratch[...].astype(BF16)


def place_kernel(
    table_ref, master_in, first_in, second_in, arrived_ref, moments_ref,
    master_ref, first_ref, second_ref, mask_ref,
):
    def step(s, carry):
        at = pl.ds(pl.multiple_of(s * ROWS, ROWS), ROWS)
        for ref, out, arrived in (
            (master_in, master_ref, lambda q: arrived_ref[q]),
            (first_in, first_ref, lambda q: moments_ref[q, 0]),
            (second_in, second_ref, lambda q: moments_ref[q, 1]),
        ):
            tile, kept = place_tile(table_ref, s, ref, arrived)
            out[at, :] = jnp.where(kept, tile, 0.0)
        mask_ref[at, :] = jnp.where(kept, 1.0, 0.0)
        return carry

    lax.fori_loop(0, SLOTS, step, 0, unroll=10)


def assemble(pieces, z, xh, weights):
    for index, piece in enumerate(pieces):
        rel, other = divmod(index, 2)
        source = lax.rem(z + rel, ZN) * 2 + lax.rem(xh + other, 2)
        at = pl.ds(pl.multiple_of(source * ROWS, ROWS), ROWS)
        weights[:, at, :] = piece[...].astype(F32).reshape(KEPT, ROWS, B)


def assemble_kernel(shards_ref, out_ref, weights):
    for i in range(2 * ZN):
        weights[:, i * ROWS : (i + 1) * ROWS, :] = shards_ref[i].astype(F32).reshape(KEPT, ROWS, B)
    out_ref[...] = weights[...].astype(BF16)


def main_kernel(*refs):
    table_ref, where_ref, upstream_in, weights_in = refs[:4]
    token_pieces = refs[4:10]
    hidden_out = refs[10]
    keep_out = refs[11:15]
    send_out = refs[15:18]
    (
        tokens_ref, upstream_ref, weights, hidden_ref, local_grad, grads, keep_ref, send_ref,
        token_sems, side_sems, out_sems,
    ) = refs[18:]
    z, xh, sign = where_ref[0], where_ref[1], where_ref[2]
    y, xl, core, y_sign = where_ref[3], where_ref[4], where_ref[5], where_ref[6]
    copies = []
    for index, ref in enumerate(token_pieces):
        other_core, step = divmod(index, 3)
        for i, rel in enumerate(Y_ORDER[step]):
            y_from = lax.rem(y + (1 - 2 * other_core) * y_sign * rel + 4, 4)
            for other_x in range(2):
                owner = (y_from * 2 + lax.rem(xl + other_x, 2)) * 2 + lax.rem(core + other_core, 2)
                copies.append(
                    pltpu.make_async_copy(
                        ref.at[2 * i + other_x], tokens_ref.at[owner], token_sems.at[len(copies)]
                    )
                )
    copies.append(pltpu.make_async_copy(weights_in, weights, side_sems.at[0]))
    copies.append(pltpu.make_async_copy(upstream_in, upstream_ref, side_sems.at[1]))
    for copy in copies:
        copy.start()
    for copy in copies:
        copy.wait()

    def block(row):
        lanes = pl.ds(pl.multiple_of(lax.rem(row, 3) * B, B), B)
        return tokens_ref[row // 3, :, lanes]

    def forward(k, carry):
        xs = [block(table_ref[BROW, table_ref[LIST, k * KEEP + j]]) for j in range(KEEP)]
        w = jnp.concatenate([weights[k * KEEP + j] for j in range(KEEP)], axis=0)
        total = jnp.dot(jnp.concatenate(xs, axis=1), w, preferred_element_type=F32)
        lanes = pl.ds(pl.multiple_of(k * B, B), B)
        square = total * total
        tangent = jnp.tanh(tanh_scale * (total + cubic_coef * square * total))
        half = 0.5 * (1.0 + tangent)
        hidden_ref[:, lanes] = (total * half).astype(BF16)
        slope = half + 0.5 * total * (1.0 - tangent * tangent) * tanh_scale * (
            1.0 + 3.0 * cubic_coef * square
        )
        local_grad[k] = (upstream_ref[:, lanes].astype(F32) * slope).astype(BF16)
        return carry

    lax.fori_loop(0, COLS, forward, 0, unroll=4)
    hidden_copy = pltpu.make_async_copy(hidden_ref, hidden_out, side_sems.at[2])
    hidden_copy.start()

    def backward(p, carry):
        for half in range(2):
            s = 2 * p + half
            x = block(table_ref[BROW, s])
            g = local_grad[table_ref[BCOL, s]]
            grads[half * B : (half + 1) * B, :] = lax.dot_general(
                x, g, (((0,), (0,)), ((), ())), preferred_element_type=F32
            )
        at = pl.ds(pl.multiple_of(p * 16, 16), 16)
        for rel in range(ZN):
            base = lax.rem(z + sign * rel + ZN, ZN) * 16

            def pair(start):
                a = grads[pl.ds(pl.multiple_of(start, ROWS), ROWS), :]
                b = grads[pl.ds(pl.multiple_of(start + B, ROWS), ROWS), :]
                return jnp.concatenate([a, b], axis=0)

            spot = ORDER.index(rel)
            keep_ref[spot, at, :] = pair(base + xh * ROWS)
            send_ref[spot, at, :] = pair(base + (1 - xh) * ROWS).astype(BF16)
        return carry

    third = SLOTS // 2 // 3

    def results(part):
        at = pl.ds(pl.multiple_of(part * third * 16, 16), third * 16)
        out = []
        for group in range(4):
            pair = pl.ds(2 * group, 2)
            out.append((keep_ref.at[pair, at, :], keep_out[group].at[:, at, :]))
            spot = pl.ds(2 if group == 3 else 0, 2)
            out.append((send_ref.at[pair, at, :], send_out[min(group, 2)].at[spot, at, :]))
        return [
            pltpu.make_async_copy(a, b, out_sems.at[part, i]) for i, (a, b) in enumerate(out)
        ]

    def chunk(part, carry):
        lax.fori_loop(0, third, lambda p, c: backward(part * third + p, c), 0, unroll=10)
        for copy in results(part):
            copy.start()
        return carry

    lax.fori_loop(0, 3, chunk, 0)
    hidden_copy.wait()

    def finish(part, carry):
        for copy in results(part):
            copy.wait()
        return carry

    lax.fori_loop(0, 3, finish, 0)


def adam_kernel(
    table_ref, own_ref, got_ref, near_ref, last_ref, mast_ref, mom_ref, var_ref, mask_ref,
    master_ref, first_ref, second_ref, copy_ref, scratch,
):
    grad = own_ref[0] + got_ref[0].astype(F32)
    grad = grad + near_ref[0].astype(F32) + last_ref[...].astype(F32)
    master = mast_ref[...]
    kept = mask_ref[...] > 0.5
    new_first = beta_one * mom_ref[...] + (1.0 - beta_one) * grad
    new_second = beta_two * var_ref[...] + (1.0 - beta_two) * grad * grad
    first_hat = new_first / (1.0 - beta_one**STEP)
    second_hat = new_second / (1.0 - beta_two**STEP)
    denominator = jnp.where(kept, jnp.sqrt(second_hat) + adam_eps, 1.0)
    master_ref[...] = jnp.where(
        kept, master - learn_rate * (first_hat / denominator + weight_decay * master), 0.0
    )
    first_ref[...] = new_first
    second_ref[...] = new_second

    def pick(i, carry):
        at = pl.ds(pl.multiple_of(table_ref[LIST, i] * ROWS, ROWS), ROWS)
        scratch[pl.ds(pl.multiple_of(i * ROWS, ROWS), ROWS), :] = master_ref[at, :]
        return carry

    lax.fori_loop(0, KEPT, pick, 0, unroll=6)
    copy_ref[...] = scratch[...].astype(BF16)


def final_kernel(*refs):
    table_ref, where_ref = refs[:2]
    pieces = refs[2:18]
    out_ref, weights = refs[18:]
    assemble(pieces, where_ref[0], where_ref[1], weights)

    def step(s, carry):
        entry = table_ref[RANK, s]
        some = (jnp.zeros((B, B), jnp.int32) + entry) < KEPT
        out_ref[s] = jnp.where(some, weights[jnp.minimum(entry, KEPT - 1)], 0.0).astype(BF16)
        return carry

    lax.fori_loop(0, SLOTS, step, 0, unroll=2)


AXES = ("dp", "tensor")
SWAP = [(i, i ^ 1) for i in range(16)]
UP = [(i, (i + 2) % 16) for i in range(16)]
DOWN = [(i, (i - 2) % 16) for i in range(16)]


def direction(z, core):
    return 1 - 2 * ((z + core) % 2)


def exchange(side):
    out = []
    for z, xh, t in itertools.product(range(ZN), range(2), range(16)):
        other = (z + side * direction(z, t % 2)) % ZN
        out.append(((z * 2 + xh) * 16 + t, (other * 2 + xh) * 16 + t))
    return out


NEAR = exchange(1)
FAR = exchange(-1)


def gather_pieces(shard):
    pieces = [[None, None] for _ in range(ZN)]
    swapped = lax.ppermute(shard, "dp", SWAP)
    up = [shard, swapped]
    down = [shard, swapped]
    pieces[0] = [shard, swapped]
    for step in range(1, 4):
        for j in range(2):
            up[j] = lax.ppermute(up[j], "dp", UP)
            down[j] = lax.ppermute(down[j], "dp", DOWN)
        for j in range(2):
            pieces[ZN - step][j] = up[j]
            pieces[step][j] = down[j]
    pieces[4][0] = lax.ppermute(up[0], "dp", UP)
    pieces[4][1] = lax.ppermute(down[1], "dp", DOWN)
    return [piece for pair in pieces for piece in pair]


def y_exchange(side):
    out = []
    for y, xl, core in itertools.product(range(4), range(2), range(2)):
        other = (y + side * direction(y, core)) % 4
        out.append(((y * 2 + xl) * 2 + core, (other * 2 + xl) * 2 + core))
    return out


Y_NEAR = y_exchange(1)
Y_FAR = y_exchange(-1)
X_SWAP = [(i, i ^ 2) for i in range(16)]
CORE_SWAP = [(i, i ^ 1) for i in range(16)]


def hop(value, pairs):
    return lax.ppermute(value, "tensor", pairs)


def reduce_chunks(keep, send):
    got = [lax.ppermute(a, "dp", SWAP) for a in send]
    got = got[:2] + [got[2][:2], got[2][2:]]

    def total(pair, more=None):
        value = keep[pair] + got[pair].astype(F32)
        return (value if more is None else value + more.astype(F32)).astype(BF16)

    a = lax.ppermute(total(0), AXES, FAR)
    b = lax.ppermute(total(1, a), AXES, NEAR)
    c = lax.ppermute(total(2, b), AXES, FAR)
    d = lax.ppermute(total(3, c)[1], AXES, NEAR)
    return keep[3], got[3], c, d


def local(tokens, upstream, master_weights, first_moment, second_moment, old_blocks, new_blocks, new_columns):
    owner = lax.axis_index("tensor")
    dp = lax.axis_index("dp")
    z = dp // 2
    me = jnp.reshape(owner, (1,)).astype(jnp.int32)
    core = owner % 2
    y = owner // 4
    spots = [z, dp % 2, direction(z, core), y, owner // 2 % 2, core, direction(y, core)]
    where = jnp.stack(spots).astype(jnp.int32)
    states = [jnp.transpose(a, (1, 0, 2)) for a in (master_weights, first_moment, second_moment)]

    swapped = hop(tokens, X_SWAP)

    table, packed, packed_moments = pl.pallas_call(
        pack_kernel,
        out_shape=(
            sd((8, 128), jnp.int32),
            sd((OWNERS * KEEP, ROWS, B), F32),
            sd((OWNERS * KEEP, 2, ROWS, B), F32),
        ),
        in_specs=[smem()] + [vmem()] * 6,
        out_specs=(vmem(),) * 3,
        scratch_shapes=[pltpu.SMEM((8, 128), jnp.int32), pltpu.SemaphoreType.DMA],
        compiler_params=params(56),
    )(me, old_blocks, new_blocks, new_columns, *states)
    arrived = lax.all_to_all(packed, "tensor", split_axis=0, concat_axis=0, tiled=True)

    arrived, swapped = lax.optimization_barrier((arrived, swapped))
    start = jnp.stack([tokens, swapped])
    near = hop(start, Y_NEAR)
    flat = sd((SLOTS * ROWS, B), F32)
    flat16 = sd((KEPT * ROWS, B), BF16)
    copies = pl.pallas_call(
        copy_in_kernel,
        out_shape=sd((2 * ZN, KEPT * ROWS, B), BF16),
        in_specs=[smem()] + [vmem()] * 2,
        out_specs=vmem(),
        scratch_shapes=[pltpu.VMEM((KEPT * ROWS, B), F32)],
        compiler_params=params(6),
    )(table, states[0], arrived)
    shards = lax.all_to_all(copies, "dp", split_axis=0, concat_axis=0, tiled=True)

    def after(value, other):
        return lax.optimization_barrier((value, other))[0]

    far = hop(jnp.concatenate([start, near], axis=0), Y_FAR)
    mine = [start, near, after(far, shards)]
    token_pieces = mine + [hop(a, CORE_SWAP) for a in mine]

    weights = pl.pallas_call(
        assemble_kernel,
        out_shape=sd((KEPT, B, B), BF16),
        in_specs=[vmem()],
        out_specs=vmem(),
        scratch_shapes=[pltpu.VMEM((KEPT, B, B), F32)],
        compiler_params=params(12),
    )(shards)
    moved_moments = lax.all_to_all(
        after(packed_moments, shards), "tensor", split_axis=0, concat_axis=0, tiled=True
    )
    pair32 = sd((2, SLOTS * ROWS, B), F32)
    pair16 = sd((2, SLOTS * ROWS, B), BF16)
    hidden_out, *pairs = pl.pallas_call(
        main_kernel,
        out_shape=(sd(upstream.shape, BF16),) + (pair32,) * 4 + (pair16,) * 2 + (sd((4, SLOTS * ROWS, B), BF16),),
        in_specs=[smem()] * 2 + [hbm()] * 8,
        out_specs=(hbm(),) * 8,
        scratch_shapes=[
            pltpu.VMEM((OWNERS,) + tokens.shape, BF16),
            pltpu.VMEM(upstream.shape, BF16),
            pltpu.VMEM((KEPT, B, B), BF16),
            pltpu.VMEM(upstream.shape, BF16),
            pltpu.VMEM((COLS, tokens.shape[0], B), BF16),
            pltpu.VMEM((2 * B, B), F32),
            pltpu.VMEM((ZN, SLOTS * ROWS, B), F32),
            pltpu.VMEM((ZN, SLOTS * ROWS, B), BF16),
            pltpu.SemaphoreType.DMA((OWNERS,)),
            pltpu.SemaphoreType.DMA((3,)),
            pltpu.SemaphoreType.DMA((3, 8)),
        ],
        compiler_params=params(56),
        cost_estimate=pl.CostEstimate(flops=4 * 10**9, bytes_accessed=2 * 10**7, transcendentals=10**6),
    )(table, where, upstream, weights, *token_pieces)
    keep, send = pairs[:4], pairs[4:]

    moved_moments, keep = lax.optimization_barrier((moved_moments, keep))
    kept_states = pl.pallas_call(
        place_kernel,
        out_shape=(flat,) * 4,
        in_specs=[smem()] + [vmem()] * 5,
        out_specs=(vmem(),) * 4,
        compiler_params=params(8),
    )(table, *states, arrived, moved_moments)

    grads = reduce_chunks(keep, send)

    new_master, new_first, new_second, fresh = pl.pallas_call(
        adam_kernel,
        out_shape=(flat, flat, flat, flat16),
        in_specs=[smem()] + [vmem()] * 8,
        out_specs=(vmem(),) * 4,
        scratch_shapes=[pltpu.VMEM((KEPT * ROWS, B), F32)],
        compiler_params=params(8),
    )(table, *grads, *kept_states)

    final = gather_pieces(fresh)
    weight_copy = pl.pallas_call(
        final_kernel,
        out_shape=sd((SLOTS, B, B), BF16),
        in_specs=[smem()] * 2 + [vmem()] * 16,
        out_specs=vmem(),
        scratch_shapes=[pltpu.VMEM((KEPT, B, B), F32)],
        compiler_params=params(12),
    )(table, where, *final)

    def back(a):
        return jnp.transpose(a.reshape(SLOTS, -1, B), (1, 0, 2))

    return (hidden_out, back(new_master), back(new_first), back(new_second), back(weight_copy))


def solution(mesh):
    split = P("dp", "tensor", None)
    return jax.shard_map(
        local,
        mesh=mesh,
        in_specs=(P("dp", "tensor"), P("dp", "tensor"), split, split, split, P(), P(), P()),
        out_specs=(P("dp", "tensor"), split, split, split, P(None, "tensor", None)),
        check_vma=False,
    )
```

```python
import itertools

import jax
import jax.numpy as jnp
from jax import lax
from jax.experimental import pallas as pl
from jax.experimental.pallas import tpu as pltpu
from jax.sharding import PartitionSpec as P

STEP = 20
tanh_scale = 0.7978845608
cubic_coef = 0.044715
beta_one = 0.9
beta_two = 0.95
adam_eps = 1e-08
learn_rate = 0.002
weight_decay = 0.1

OWNERS = 16
SLOTS = 60
KEEP = 3
COLS = 12
KEPT = COLS * KEEP
B = 128
ROWS = 8
NBC = 192
ZN = 8
F32 = jnp.float32
BF16 = jnp.bfloat16


def params(mib):
    return pltpu.CompilerParams(vmem_limit_bytes=mib * 1024 * 1024)

Z_ORDER = ((0,), (1,), (-1, -2), (2, 3), (-3, -4))
Y_ORDER = ((0,), (1,), (-1, -2))

ORDER = (5, 4, 2, 3, 7, 6, 0, 1)

SEND, PLACE, BROW, BCOL, LIST, RANK = range(6)


def vmem():
    return pl.BlockSpec(memory_space=pltpu.VMEM)


def hbm():
    return pl.BlockSpec(memory_space=pltpu.HBM)


def anywhere():
    return pl.BlockSpec(memory_space=pl.ANY)


def smem():
    return pl.BlockSpec(memory_space=pltpu.SMEM)


def sd(shape, dtype):
    return jax.ShapeDtypeStruct(shape, dtype)


def routing_table(me, old_ref, new_ref, cols_ref):
    n = SLOTS
    sub = lax.broadcasted_iota(jnp.int32, (n, n), 0)
    lane = lax.broadcasted_iota(jnp.int32, (n, n), 1)
    eye = sub == lane
    wide = lax.broadcasted_iota(jnp.int32, (n, 128), 1).astype(F32)
    slot = lax.broadcasted_iota(jnp.int32, (n, 128), 0).astype(F32)

    def to_col(row):
        return jnp.sum(jnp.where(eye, row, 0.0), axis=1, keepdims=True)

    def to_row(col):
        return jnp.sum(jnp.where(eye, col, 0.0), axis=0, keepdims=True)

    old_all = old_ref[...].astype(F32)
    new_all = new_ref[...].astype(F32)
    old_row = old_ref[pl.ds(me, 1), :].astype(F32)
    new_row = new_ref[pl.ds(me, 1), :].astype(F32)
    old_col = to_col(old_row)
    new_col = to_col(new_row)
    lane_f = lane.astype(F32)
    me_f = me.astype(F32) + 1.0
    zero = jnp.zeros((n, n), F32)
    target = zero
    source = zero
    source_slot = zero
    for o in range(OWNERS):
        target = target + jnp.where(old_col == new_all[o : o + 1, :], o + 1.0, 0.0)
        hit = new_col == old_all[o : o + 1, :]
        source = source + jnp.where(hit, o + 1.0, 0.0)
        source_slot = source_slot + jnp.where(hit, lane_f, 0.0)
    target = jnp.sum(target, axis=1, keepdims=True)
    source = jnp.sum(source, axis=1, keepdims=True)
    source_slot = jnp.sum(source_slot, axis=1, keepdims=True)

    def rank(kind_col, id_row, id_col):
        same = (to_row(kind_col) == kind_col) & (id_row < id_col)
        return jnp.sum(jnp.where(same, 1.0, 0.0), axis=1, keepdims=True)

    def listing(entry_col):
        return n + jnp.sum(jnp.where(entry_col == wide, slot - n, 0.0), axis=0, keepdims=True)

    moving = (target > 0.0) & (target != me_f)
    packet = jnp.where(moving, (target - 1.0) * KEEP + rank(target, old_row, old_col), -1.0)

    arrived = n + 1.0 + (source - 1.0) * KEEP + rank(source, new_row, new_col)
    kept = source > 0.0
    place = jnp.where(kept, jnp.where(source == me_f, source_slot, arrived), float(n))

    block_row = jnp.floor((new_col + 0.5) * (1.0 / NBC))
    block_col = new_col - block_row * NBC
    mine = cols_ref[pl.ds(me, 1), :].astype(F32)
    order = lax.broadcasted_iota(jnp.int32, (n, COLS), 1).astype(F32)
    kth = jnp.sum(jnp.where(block_col == mine, order, 0.0), axis=1, keepdims=True)
    kept_kth = jnp.where(kept, kth, -1.0)
    within = rank(kept_kth, lane_f[0:1, :], slot[:, 0:1])
    entry = jnp.where(kept, kth * KEEP + within, float(KEPT))

    def spread(col):
        return jnp.sum(jnp.where(slot == wide, col, 0.0), axis=0, keepdims=True)

    return [
        listing(packet), spread(place), spread(block_row), spread(kth), listing(entry), spread(entry),
    ]


def pack_kernel(
    old_ref, new_ref, cols_ref, master_ref, first_ref, second_ref, table_ref, out_ref, moments_ref, scalars, sem
):
    rows = routing_table(lax.axis_index("tensor"), old_ref, new_ref, cols_ref)
    for i, row in enumerate(rows):
        table_ref[i : i + 1, :] = row.astype(jnp.int32)
    table_ref[len(rows) : 8, :] = jnp.zeros((8 - len(rows), 128), jnp.int32)
    copy = pltpu.make_async_copy(table_ref, scalars, sem)
    copy.start()
    copy.wait()

    def step(q, carry):
        slot = scalars[SEND, q]
        at = jnp.minimum(slot, SLOTS - 1)
        some = (jnp.zeros((ROWS, B), jnp.int32) + slot) < SLOTS
        out_ref[q] = jnp.where(some, master_ref[at], 0.0)
        for state, ref in enumerate((first_ref, second_ref)):
            moments_ref[q, state] = jnp.where(some, ref[at], 0.0)
        return carry

    lax.fori_loop(0, OWNERS * KEEP, step, 0, unroll=8)


def place_tile(table_ref, slot, ref, arrived):
    index = table_ref[PLACE, slot]
    tag = jnp.zeros((ROWS, B), jnp.int32) + index
    here = ref[jnp.minimum(index, SLOTS - 1)]
    there = arrived(jnp.maximum(index - SLOTS - 1, 0))
    return jnp.where(tag < SLOTS, here, there), tag != SLOTS


def copy_in_kernel(table_ref, master_in, arrived_ref, copy_ref, scratch):
    def step(i, carry):
        tile, _ = place_tile(table_ref, table_ref[LIST, i], master_in, lambda at: arrived_ref[at])
        scratch[pl.ds(pl.multiple_of(i * ROWS, ROWS), ROWS), :] = tile
        return carry

    lax.fori_loop(0, KEPT, step, 0, unroll=12)
    copy_ref[...] = scratch[...].astype(BF16)


def place_kernel(
    table_ref, master_in, first_in, second_in, arrived_ref, moments_ref,
    master_ref, first_ref, second_ref, mask_ref,
):
    def step(s, carry):
        at = pl.ds(pl.multiple_of(s * ROWS, ROWS), ROWS)
        for ref, out, arrived in (
            (master_in, master_ref, lambda q: arrived_ref[q]),
            (first_in, first_ref, lambda q: moments_ref[q, 0]),
            (second_in, second_ref, lambda q: moments_ref[q, 1]),
        ):
            tile, kept = place_tile(table_ref, s, ref, arrived)
            out[at, :] = jnp.where(kept, tile, 0.0)
        mask_ref[at, :] = jnp.where(kept, 1.0, 0.0)
        return carry

    lax.fori_loop(0, SLOTS, step, 0, unroll=10)


def place_of(axis):
    index = lax.axis_index(axis)
    return index // 2, index % 2


def assemble(pieces, z, xh, weights):
    for index, piece in enumerate(pieces):
        rel, other = divmod(index, 2)
        source = lax.rem(z + rel, ZN) * 2 + lax.rem(xh + other, 2)
        at = pl.ds(pl.multiple_of(source * ROWS, ROWS), ROWS)
        weights[:, at, :] = piece[...].astype(F32).reshape(KEPT, ROWS, B)


def assemble_kernel(*refs):
    pieces = refs[:5]
    out_ref, weights = refs[5:]
    z, xh = place_of("dp")
    sign = direction(z, lax.axis_index("tensor") % 2)
    for ref, rels in zip(pieces, Z_ORDER, strict=True):
        for i, rel in enumerate(rels):
            for other in range(2):
                source = lax.rem(z + sign * rel + ZN, ZN) * 2 + lax.rem(xh + other, 2)
                at = pl.ds(pl.multiple_of(source * ROWS, ROWS), ROWS)
                weights[:, at, :] = ref[2 * i + other].astype(F32).reshape(KEPT, ROWS, B)
    out_ref[...] = weights[...].astype(BF16)


def main_kernel(*refs):
    table_ref, upstream_in, weights = refs[:3]
    token_pieces = refs[3:9]
    hidden_out = refs[9]
    keep_out = refs[10:14]
    send_out = refs[14:17]
    (
        tokens_ref, upstream_ref, hidden_ref, local_grad, grads, keep_ref, send_ref,
        token_sems, side_sems, out_sems,
    ) = refs[17:]
    z, xh = place_of("dp")
    y, rest = lax.axis_index("tensor") // 4, lax.axis_index("tensor") % 4
    xl, core = rest // 2, rest % 2
    sign, y_sign = direction(z, core), direction(y, core)
    copies = []
    for index, ref in enumerate(token_pieces):
        other_core, step = divmod(index, 3)
        for i, rel in enumerate(Y_ORDER[step]):
            y_from = lax.rem(y + (1 - 2 * other_core) * y_sign * rel + 4, 4)
            for other_x in range(2):
                owner = (y_from * 2 + lax.rem(xl + other_x, 2)) * 2 + lax.rem(core + other_core, 2)
                copies.append(
                    pltpu.make_async_copy(
                        ref.at[2 * i + other_x], tokens_ref.at[owner], token_sems.at[len(copies)]
                    )
                )
    copies.append(pltpu.make_async_copy(upstream_in, upstream_ref, side_sems.at[0]))
    for copy in copies:
        copy.start()
    for copy in copies:
        copy.wait()

    def block(row):
        lanes = pl.ds(pl.multiple_of(lax.rem(row, 3) * B, B), B)
        return tokens_ref[row // 3, :, lanes]

    def forward(k, carry):
        xs = [block(table_ref[BROW, table_ref[LIST, k * KEEP + j]]) for j in range(KEEP)]
        w = jnp.concatenate([weights[k * KEEP + j] for j in range(KEEP)], axis=0)
        total = jnp.dot(jnp.concatenate(xs, axis=1), w, preferred_element_type=F32)
        lanes = pl.ds(pl.multiple_of(k * B, B), B)
        square = total * total
        tangent = jnp.tanh(tanh_scale * (total + cubic_coef * square * total))
        half = 0.5 * (1.0 + tangent)
        hidden_ref[:, lanes] = (total * half).astype(BF16)
        slope = half + 0.5 * total * (1.0 - tangent * tangent) * tanh_scale * (
            1.0 + 3.0 * cubic_coef * square
        )
        local_grad[k] = (upstream_ref[:, lanes].astype(F32) * slope).astype(BF16)
        return carry

    lax.fori_loop(0, COLS, forward, 0, unroll=4)
    hidden_copy = pltpu.make_async_copy(hidden_ref, hidden_out, side_sems.at[1])
    hidden_copy.start()

    def backward(p, carry):
        for half in range(2):
            s = 2 * p + half
            x = block(table_ref[BROW, s])
            g = local_grad[table_ref[BCOL, s]]
            grads[half * B : (half + 1) * B, :] = lax.dot_general(
                x, g, (((0,), (0,)), ((), ())), preferred_element_type=F32
            )
        at = pl.ds(pl.multiple_of(p * 16, 16), 16)
        for rel in range(ZN):
            base = lax.rem(z + sign * rel + ZN, ZN) * 16

            def pair(start):
                a = grads[pl.ds(pl.multiple_of(start, ROWS), ROWS), :]
                b = grads[pl.ds(pl.multiple_of(start + B, ROWS), ROWS), :]
                return jnp.concatenate([a, b], axis=0)

            spot = ORDER.index(rel)
            keep_ref[spot, at, :] = pair(base + xh * ROWS)
            send_ref[spot, at, :] = pair(base + (1 - xh) * ROWS).astype(BF16)
        return carry

    third = SLOTS // 2 // 3

    def results(part):
        at = pl.ds(pl.multiple_of(part * third * 16, 16), third * 16)
        out = []
        for group in range(4):
            pair = pl.ds(2 * group, 2)
            out.append((keep_ref.at[pair, at, :], keep_out[group].at[:, at, :]))
            spot = pl.ds(2 if group == 3 else 0, 2)
            out.append((send_ref.at[pair, at, :], send_out[min(group, 2)].at[spot, at, :]))
        return [
            pltpu.make_async_copy(a, b, out_sems.at[part, i]) for i, (a, b) in enumerate(out)
        ]

    def chunk(part, carry):
        lax.fori_loop(0, third, lambda p, c: backward(part * third + p, c), 0, unroll=10)
        for copy in results(part):
            copy.start()
        return carry

    lax.fori_loop(0, 3, chunk, 0)
    hidden_copy.wait()

    def finish(part, carry):
        for copy in results(part):
            copy.wait()
        return carry

    lax.fori_loop(0, 3, finish, 0)


def adam_kernel(
    table_ref, own_ref, got_ref, near_ref, last_ref, mast_ref, mom_ref, var_ref, mask_ref,
    master_ref, first_ref, second_ref, copy_ref, scratch,
):
    grad = own_ref[0] + got_ref[0].astype(F32)
    grad = grad + near_ref[0].astype(F32) + last_ref[...].astype(F32)
    master = mast_ref[...]
    kept = mask_ref[...] > 0.5
    new_first = beta_one * mom_ref[...] + (1.0 - beta_one) * grad
    new_second = beta_two * var_ref[...] + (1.0 - beta_two) * grad * grad
    first_hat = new_first / (1.0 - beta_one**STEP)
    second_hat = new_second / (1.0 - beta_two**STEP)
    denominator = jnp.where(kept, jnp.sqrt(second_hat) + adam_eps, 1.0)
    master_ref[...] = jnp.where(
        kept, master - learn_rate * (first_hat / denominator + weight_decay * master), 0.0
    )
    first_ref[...] = new_first
    second_ref[...] = new_second

    def pick(i, carry):
        at = pl.ds(pl.multiple_of(table_ref[LIST, i] * ROWS, ROWS), ROWS)
        scratch[pl.ds(pl.multiple_of(i * ROWS, ROWS), ROWS), :] = master_ref[at, :]
        return carry

    lax.fori_loop(0, KEPT, pick, 0, unroll=6)
    copy_ref[...] = scratch[...].astype(BF16)


def final_kernel(*refs):
    table_ref = refs[0]
    pieces = refs[1:17]
    out_ref, weights = refs[17:]
    assemble(pieces, *place_of("dp"), weights)

    def step(s, carry):
        entry = table_ref[RANK, s]
        some = (jnp.zeros((B, B), jnp.int32) + entry) < KEPT
        out_ref[s] = jnp.where(some, weights[jnp.minimum(entry, KEPT - 1)], 0.0).astype(BF16)
        return carry

    lax.fori_loop(0, SLOTS, step, 0, unroll=2)


AXES = ("dp", "tensor")
SWAP = [(i, i ^ 1) for i in range(16)]
UP = [(i, (i + 2) % 16) for i in range(16)]
DOWN = [(i, (i - 2) % 16) for i in range(16)]


def direction(z, core):
    return 1 - 2 * ((z + core) % 2)


def exchange(side):
    out = []
    for z, xh, t in itertools.product(range(ZN), range(2), range(16)):
        other = (z + side * direction(z, t % 2)) % ZN
        out.append(((z * 2 + xh) * 16 + t, (other * 2 + xh) * 16 + t))
    return out


NEAR = exchange(1)
FAR = exchange(-1)


def gather_pieces(shard):
    pieces = [[None, None] for _ in range(ZN)]
    swapped = lax.ppermute(shard, "dp", SWAP)
    up = [shard, swapped]
    down = [shard, swapped]
    pieces[0] = [shard, swapped]
    for step in range(1, 4):
        for j in range(2):
            up[j] = lax.ppermute(up[j], "dp", UP)
            down[j] = lax.ppermute(down[j], "dp", DOWN)
        for j in range(2):
            pieces[ZN - step][j] = up[j]
            pieces[step][j] = down[j]
    pieces[4][0] = lax.ppermute(up[0], "dp", UP)
    pieces[4][1] = lax.ppermute(down[1], "dp", DOWN)
    return [piece for pair in pieces for piece in pair]


def y_exchange(side):
    out = []
    for y, xl, core in itertools.product(range(4), range(2), range(2)):
        other = (y + side * direction(y, core)) % 4
        out.append(((y * 2 + xl) * 2 + core, (other * 2 + xl) * 2 + core))
    return out


Y_NEAR = y_exchange(1)
Y_FAR = y_exchange(-1)
X_SWAP = [(i, i ^ 2) for i in range(16)]
CORE_SWAP = [(i, i ^ 1) for i in range(16)]


def hop(value, pairs):
    return lax.ppermute(value, "tensor", pairs)


def reduce_chunks(keep, send):
    got = [lax.ppermute(a, "dp", SWAP) for a in send]
    got = got[:2] + [got[2][:2], got[2][2:]]

    def total(pair, more=None):
        value = keep[pair] + got[pair].astype(F32)
        return (value if more is None else value + more.astype(F32)).astype(BF16)

    a = lax.ppermute(total(0), AXES, FAR)
    b = lax.ppermute(total(1, a), AXES, NEAR)
    c = lax.ppermute(total(2, b), AXES, FAR)
    d = lax.ppermute(total(3, c)[1], AXES, NEAR)
    return keep[3], got[3], c, d


def local(tokens, upstream, master_weights, first_moment, second_moment, old_blocks, new_blocks, new_columns):
    states = [jnp.transpose(a, (1, 0, 2)) for a in (master_weights, first_moment, second_moment)]

    swapped = hop(tokens, X_SWAP)

    table, packed, packed_moments = pl.pallas_call(
        pack_kernel,
        out_shape=(
            sd((8, 128), jnp.int32),
            sd((OWNERS * KEEP, ROWS, B), F32),
            sd((OWNERS * KEEP, 2, ROWS, B), F32),
        ),
        in_specs=[vmem()] * 6,
        out_specs=(vmem(),) * 3,
        scratch_shapes=[pltpu.SMEM((8, 128), jnp.int32), pltpu.SemaphoreType.DMA],
        compiler_params=params(56),
    )(old_blocks, new_blocks, new_columns, *states)
    arrived = lax.all_to_all(packed, "tensor", split_axis=0, concat_axis=0, tiled=True)

    arrived, swapped = lax.optimization_barrier((arrived, swapped))
    start = jnp.stack([tokens, swapped])
    near = hop(start, Y_NEAR)
    flat = sd((SLOTS * ROWS, B), F32)
    flat16 = sd((KEPT * ROWS, B), BF16)
    copy_in = pl.pallas_call(
        copy_in_kernel,
        out_shape=flat16,
        in_specs=[smem()] + [vmem()] * 2,
        out_specs=vmem(),
        scratch_shapes=[pltpu.VMEM((KEPT * ROWS, B), F32)],
        compiler_params=params(6),
    )(table, states[0], arrived)
    pair = jnp.stack([copy_in, lax.ppermute(copy_in, "dp", SWAP)])
    shards = [pair, lax.ppermute(pair, AXES, NEAR)]
    shards.append(lax.ppermute(jnp.concatenate(shards, axis=0), AXES, FAR))
    shards.append(lax.ppermute(shards[2], AXES, NEAR))
    shards.append(lax.ppermute(shards[3], AXES, FAR))

    def after(value, other):
        return lax.optimization_barrier((value, other))[0]

    far = hop(jnp.concatenate([start, after(near, shards[1])], axis=0), Y_FAR)
    mine = [start, near, after(far, shards[4])]
    token_pieces = mine + [hop(a, CORE_SWAP) for a in mine]

    weights = pl.pallas_call(
        assemble_kernel,
        out_shape=sd((KEPT, B, B), BF16),
        in_specs=[vmem()] * 5,
        out_specs=vmem(),
        scratch_shapes=[pltpu.VMEM((KEPT, B, B), F32)],
        compiler_params=params(12),
    )(*shards)
    moved_moments = lax.all_to_all(
        after(packed_moments, shards[4]), "tensor", split_axis=0, concat_axis=0, tiled=True
    )
    pair32 = sd((2, SLOTS * ROWS, B), F32)
    pair16 = sd((2, SLOTS * ROWS, B), BF16)
    hidden_out, *pairs = pl.pallas_call(
        main_kernel,
        out_shape=(sd(upstream.shape, BF16),) + (pair32,) * 4 + (pair16,) * 2 + (sd((4, SLOTS * ROWS, B), BF16),),
        in_specs=[smem()] + [hbm(), vmem()] + [anywhere()] * 6,
        out_specs=(hbm(),) * 8,
        scratch_shapes=[
            pltpu.VMEM((OWNERS,) + tokens.shape, BF16),
            pltpu.VMEM(upstream.shape, BF16),
            pltpu.VMEM(upstream.shape, BF16),
            pltpu.VMEM((COLS, tokens.shape[0], B), BF16),
            pltpu.VMEM((2 * B, B), F32),
            pltpu.VMEM((ZN, SLOTS * ROWS, B), F32),
            pltpu.VMEM((ZN, SLOTS * ROWS, B), BF16),
            pltpu.SemaphoreType.DMA((OWNERS,)),
            pltpu.SemaphoreType.DMA((2,)),
            pltpu.SemaphoreType.DMA((3, 8)),
        ],
        compiler_params=params(56),
        cost_estimate=pl.CostEstimate(flops=4 * 10**9, bytes_accessed=2 * 10**7, transcendentals=10**6),
    )(table, upstream, weights, *token_pieces)
    keep, send = pairs[:4], pairs[4:]

    moved_moments, keep = lax.optimization_barrier((moved_moments, keep))
    kept_states = pl.pallas_call(
        place_kernel,
        out_shape=(flat,) * 4,
        in_specs=[smem()] + [vmem()] * 5,
        out_specs=(vmem(),) * 4,
        compiler_params=params(8),
    )(table, *states, arrived, moved_moments)

    grads = reduce_chunks(keep, send)

    new_master, new_first, new_second, fresh = pl.pallas_call(
        adam_kernel,
        out_shape=(flat, flat, flat, flat16),
        in_specs=[smem()] + [vmem()] * 8,
        out_specs=(vmem(),) * 4,
        scratch_shapes=[pltpu.VMEM((KEPT * ROWS, B), F32)],
        compiler_params=params(8),
    )(table, *grads, *kept_states)

    final = gather_pieces(fresh)
    weight_copy = pl.pallas_call(
        final_kernel,
        out_shape=sd((SLOTS, B, B), BF16),
        in_specs=[smem()] + [vmem()] * 16,
        out_specs=vmem(),
        scratch_shapes=[pltpu.VMEM((KEPT, B, B), F32)],
        compiler_params=params(12),
    )(table, *final)

    def back(a):
        return jnp.transpose(a.reshape(SLOTS, -1, B), (1, 0, 2))

    return (hidden_out, back(new_master), back(new_first), back(new_second), back(weight_copy))


def solution(mesh):
    split = P("dp", "tensor", None)
    return jax.shard_map(
        local,
        mesh=mesh,
        in_specs=(P("dp", "tensor"), P("dp", "tensor"), split, split, split, P(), P(), P()),
        out_specs=(P("dp", "tensor"), split, split, split, P(None, "tensor", None)),
        check_vma=False,
    )
```

```python
import itertools

import jax
import jax.numpy as jnp
from jax import lax
from jax.experimental import pallas as pl
from jax.experimental.pallas import tpu as pltpu
from jax.sharding import PartitionSpec as P

STEP = 20
tanh_scale = 0.7978845608
cubic_coef = 0.044715
beta_one = 0.9
beta_two = 0.95
adam_eps = 1e-08
learn_rate = 0.002
weight_decay = 0.1

OWNERS = 16
SLOTS = 60
KEEP = 3
COLS = 12
KEPT = COLS * KEEP
B = 128
ROWS = 8
NBC = 192
ZN = 8
F32 = jnp.float32
BF16 = jnp.bfloat16


def params(mib):
    return pltpu.CompilerParams(vmem_limit_bytes=mib * 1024 * 1024)

Z_ORDER = ((0,), (1,), (-1, -2), (2, 3), (-3, -4))
Y_ORDER = ((0,), (1,), (-1, -2))

ORDER = (5, 4, 2, 3, 7, 6, 0, 1)

SEND, PLACE, BROW, BCOL, LIST, RANK = range(6)


def vmem():
    return pl.BlockSpec(memory_space=pltpu.VMEM)


def hbm():
    return pl.BlockSpec(memory_space=pltpu.HBM)


def anywhere():
    return pl.BlockSpec(memory_space=pl.ANY)


def smem():
    return pl.BlockSpec(memory_space=pltpu.SMEM)


def sd(shape, dtype):
    return jax.ShapeDtypeStruct(shape, dtype)


def routing_table(me, old_ref, new_ref, cols_ref):
    n = SLOTS
    sub = lax.broadcasted_iota(jnp.int32, (n, n), 0)
    lane = lax.broadcasted_iota(jnp.int32, (n, n), 1)
    eye = sub == lane
    wide = lax.broadcasted_iota(jnp.int32, (n, 128), 1).astype(F32)
    slot = lax.broadcasted_iota(jnp.int32, (n, 128), 0).astype(F32)

    def to_col(row):
        return jnp.sum(jnp.where(eye, row, 0.0), axis=1, keepdims=True)

    def to_row(col):
        return jnp.sum(jnp.where(eye, col, 0.0), axis=0, keepdims=True)

    old_all = old_ref[...].astype(F32)
    new_all = new_ref[...].astype(F32)
    old_row = old_ref[pl.ds(me, 1), :].astype(F32)
    new_row = new_ref[pl.ds(me, 1), :].astype(F32)
    old_col = to_col(old_row)
    new_col = to_col(new_row)
    lane_f = lane.astype(F32)
    me_f = me.astype(F32) + 1.0
    zero = jnp.zeros((n, n), F32)
    target = zero
    source = zero
    source_slot = zero
    for o in range(OWNERS):
        target = target + jnp.where(old_col == new_all[o : o + 1, :], o + 1.0, 0.0)
        hit = new_col == old_all[o : o + 1, :]
        source = source + jnp.where(hit, o + 1.0, 0.0)
        source_slot = source_slot + jnp.where(hit, lane_f, 0.0)
    target = jnp.sum(target, axis=1, keepdims=True)
    source = jnp.sum(source, axis=1, keepdims=True)
    source_slot = jnp.sum(source_slot, axis=1, keepdims=True)

    def rank(kind_col, id_row, id_col):
        same = (to_row(kind_col) == kind_col) & (id_row < id_col)
        return jnp.sum(jnp.where(same, 1.0, 0.0), axis=1, keepdims=True)

    def listing(entry_col):
        return n + jnp.sum(jnp.where(entry_col == wide, slot - n, 0.0), axis=0, keepdims=True)

    moving = (target > 0.0) & (target != me_f)
    packet = jnp.where(moving, (target - 1.0) * KEEP + rank(target, old_row, old_col), -1.0)

    arrived = n + 1.0 + (source - 1.0) * KEEP + rank(source, new_row, new_col)
    kept = source > 0.0
    place = jnp.where(kept, jnp.where(source == me_f, source_slot, arrived), float(n))

    block_row = jnp.floor((new_col + 0.5) * (1.0 / NBC))
    block_col = new_col - block_row * NBC
    mine = cols_ref[pl.ds(me, 1), :].astype(F32)
    order = lax.broadcasted_iota(jnp.int32, (n, COLS), 1).astype(F32)
    kth = jnp.sum(jnp.where(block_col == mine, order, 0.0), axis=1, keepdims=True)
    kept_kth = jnp.where(kept, kth, -1.0)
    within = rank(kept_kth, lane_f[0:1, :], slot[:, 0:1])
    entry = jnp.where(kept, kth * KEEP + within, float(KEPT))

    def spread(col):
        return jnp.sum(jnp.where(slot == wide, col, 0.0), axis=0, keepdims=True)

    return [
        listing(packet), spread(place), spread(block_row), spread(kth), listing(entry), spread(entry),
    ]


def pack(table_ref, pairs):
    def step(q, carry):
        slot = table_ref[SEND, q]
        at = jnp.minimum(slot, SLOTS - 1)
        some = (jnp.zeros((ROWS, B), jnp.int32) + slot) < SLOTS
        for ref, out in pairs:
            out[q] = jnp.where(some, ref[at], 0.0)
        return carry

    lax.fori_loop(0, OWNERS * KEEP, step, 0, unroll=8)


def pack_kernel(old_ref, new_ref, cols_ref, master_ref, table_ref, out_ref, scalars, sem):
    rows = routing_table(lax.axis_index("tensor"), old_ref, new_ref, cols_ref)
    for i, row in enumerate(rows):
        table_ref[i : i + 1, :] = row.astype(jnp.int32)
    table_ref[len(rows) : 8, :] = jnp.zeros((8 - len(rows), 128), jnp.int32)
    copy = pltpu.make_async_copy(table_ref, scalars, sem)
    copy.start()
    copy.wait()
    pack(scalars, [(master_ref, out_ref)])


def pack_moments_kernel(table_ref, first_ref, second_ref, out_ref):
    pack(table_ref, [(first_ref, out_ref.at[:, 0]), (second_ref, out_ref.at[:, 1])])


def place_tile(table_ref, slot, ref, arrived):
    index = table_ref[PLACE, slot]
    tag = jnp.zeros((ROWS, B), jnp.int32) + index
    here = ref[jnp.minimum(index, SLOTS - 1)]
    there = arrived(jnp.maximum(index - SLOTS - 1, 0))
    return jnp.where(tag < SLOTS, here, there), tag != SLOTS


def copy_in_kernel(table_ref, master_in, arrived_ref, copy_ref, scratch):
    def step(i, carry):
        tile, _ = place_tile(table_ref, table_ref[LIST, i], master_in, lambda at: arrived_ref[at])
        scratch[pl.ds(pl.multiple_of(i * ROWS, ROWS), ROWS), :] = tile
        return carry

    lax.fori_loop(0, KEPT, step, 0, unroll=12)
    copy_ref[...] = scratch[...].astype(BF16)


def place_kernel(
    table_ref, master_in, first_in, second_in, arrived_ref, moments_ref,
    master_ref, first_ref, second_ref, mask_ref,
):
    def step(s, carry):
        at = pl.ds(pl.multiple_of(s * ROWS, ROWS), ROWS)
        for ref, out, arrived in (
            (master_in, master_ref, lambda q: arrived_ref[q]),
            (first_in, first_ref, lambda q: moments_ref[q, 0]),
            (second_in, second_ref, lambda q: moments_ref[q, 1]),
        ):
            tile, kept = place_tile(table_ref, s, ref, arrived)
            out[at, :] = jnp.where(kept, tile, 0.0)
        mask_ref[at, :] = jnp.where(kept, 1.0, 0.0)
        return carry

    lax.fori_loop(0, SLOTS, step, 0, unroll=10)


def place_of(axis):
    index = lax.axis_index(axis)
    return index // 2, index % 2


def assemble(pieces, z, xh, weights):
    for index, piece in enumerate(pieces):
        rel, other = divmod(index, 2)
        source = lax.rem(z + rel, ZN) * 2 + lax.rem(xh + other, 2)
        at = pl.ds(pl.multiple_of(source * ROWS, ROWS), ROWS)
        weights[:, at, :] = piece[...].astype(F32).reshape(KEPT, ROWS, B)


def assemble_kernel(*refs):
    pieces = refs[:5]
    out_ref, weights = refs[5:]
    z, xh = place_of("dp")
    sign = direction(z, lax.axis_index("tensor") % 2)
    for ref, rels in zip(pieces, Z_ORDER, strict=True):
        for i, rel in enumerate(rels):
            for other in range(2):
                source = lax.rem(z + sign * rel + ZN, ZN) * 2 + lax.rem(xh + other, 2)
                at = pl.ds(pl.multiple_of(source * ROWS, ROWS), ROWS)
                weights[:, at, :] = ref[2 * i + other].astype(F32).reshape(KEPT, ROWS, B)
    out_ref[...] = weights[...].astype(BF16)


def main_kernel(*refs):
    table_ref, upstream_in, weights = refs[:3]
    token_pieces = refs[3:9]
    hidden_out = refs[9]
    keep_out = refs[10:14]
    send_out = refs[14:17]
    (
        tokens_ref, upstream_ref, hidden_ref, local_grad, grads, keep_ref, send_ref,
        token_sems, side_sems, out_sems,
    ) = refs[17:]
    z, xh = place_of("dp")
    y, rest = lax.axis_index("tensor") // 4, lax.axis_index("tensor") % 4
    xl, core = rest // 2, rest % 2
    sign, y_sign = direction(z, core), direction(y, core)
    copies = []
    for index, ref in enumerate(token_pieces):
        other_core, step = divmod(index, 3)
        for i, rel in enumerate(Y_ORDER[step]):
            y_from = lax.rem(y + (1 - 2 * other_core) * y_sign * rel + 4, 4)
            for other_x in range(2):
                owner = (y_from * 2 + lax.rem(xl + other_x, 2)) * 2 + lax.rem(core + other_core, 2)
                copies.append(
                    pltpu.make_async_copy(
                        ref.at[2 * i + other_x], tokens_ref.at[owner], token_sems.at[len(copies)]
                    )
                )
    copies.append(pltpu.make_async_copy(upstream_in, upstream_ref, side_sems.at[0]))
    for copy in copies:
        copy.start()
    for copy in copies:
        copy.wait()

    def block(row):
        lanes = pl.ds(pl.multiple_of(lax.rem(row, 3) * B, B), B)
        return tokens_ref[row // 3, :, lanes]

    def forward(k, carry):
        xs = [block(table_ref[BROW, table_ref[LIST, k * KEEP + j]]) for j in range(KEEP)]
        w = jnp.concatenate([weights[k * KEEP + j] for j in range(KEEP)], axis=0)
        total = jnp.dot(jnp.concatenate(xs, axis=1), w, preferred_element_type=F32)
        lanes = pl.ds(pl.multiple_of(k * B, B), B)
        square = total * total
        tangent = jnp.tanh(tanh_scale * (total + cubic_coef * square * total))
        half = 0.5 * (1.0 + tangent)
        hidden_ref[:, lanes] = (total * half).astype(BF16)
        slope = half + 0.5 * total * (1.0 - tangent * tangent) * tanh_scale * (
            1.0 + 3.0 * cubic_coef * square
        )
        local_grad[k] = (upstream_ref[:, lanes].astype(F32) * slope).astype(BF16)
        return carry

    lax.fori_loop(0, COLS, forward, 0, unroll=4)
    hidden_copy = pltpu.make_async_copy(hidden_ref, hidden_out, side_sems.at[1])
    hidden_copy.start()

    def backward(p, carry):
        for half in range(2):
            s = 2 * p + half
            x = block(table_ref[BROW, s])
            g = local_grad[table_ref[BCOL, s]]
            grads[half * B : (half + 1) * B, :] = lax.dot_general(
                x, g, (((0,), (0,)), ((), ())), preferred_element_type=F32
            )
        at = pl.ds(pl.multiple_of(p * 16, 16), 16)
        for rel in range(ZN):
            base = lax.rem(z + sign * rel + ZN, ZN) * 16

            def pair(start):
                a = grads[pl.ds(pl.multiple_of(start, ROWS), ROWS), :]
                b = grads[pl.ds(pl.multiple_of(start + B, ROWS), ROWS), :]
                return jnp.concatenate([a, b], axis=0)

            spot = ORDER.index(rel)
            keep_ref[spot, at, :] = pair(base + xh * ROWS)
            send_ref[spot, at, :] = pair(base + (1 - xh) * ROWS).astype(BF16)
        return carry

    third = SLOTS // 2 // 3

    def results(part):
        at = pl.ds(pl.multiple_of(part * third * 16, 16), third * 16)
        out = []
        for group in range(4):
            pair = pl.ds(2 * group, 2)
            out.append((keep_ref.at[pair, at, :], keep_out[group].at[:, at, :]))
            spot = pl.ds(2 if group == 3 else 0, 2)
            out.append((send_ref.at[pair, at, :], send_out[min(group, 2)].at[spot, at, :]))
        return [
            pltpu.make_async_copy(a, b, out_sems.at[part, i]) for i, (a, b) in enumerate(out)
        ]

    def chunk(part, carry):
        lax.fori_loop(0, third, lambda p, c: backward(part * third + p, c), 0, unroll=10)
        for copy in results(part):
            copy.start()
        return carry

    lax.fori_loop(0, 3, chunk, 0)
    hidden_copy.wait()

    def finish(part, carry):
        for copy in results(part):
            copy.wait()
        return carry

    lax.fori_loop(0, 3, finish, 0)


def adam_kernel(
    table_ref, own_ref, got_ref, near_ref, last_ref, mast_ref, mom_ref, var_ref, mask_ref,
    master_ref, first_ref, second_ref, copy_ref, scratch,
):
    grad = own_ref[0] + got_ref[0].astype(F32)
    grad = grad + near_ref[0].astype(F32) + last_ref[...].astype(F32)
    master = mast_ref[...]
    kept = mask_ref[...] > 0.5
    new_first = beta_one * mom_ref[...] + (1.0 - beta_one) * grad
    new_second = beta_two * var_ref[...] + (1.0 - beta_two) * grad * grad
    first_hat = new_first / (1.0 - beta_one**STEP)
    second_hat = new_second / (1.0 - beta_two**STEP)
    denominator = jnp.where(kept, jnp.sqrt(second_hat) + adam_eps, 1.0)
    master_ref[...] = jnp.where(
        kept, master - learn_rate * (first_hat / denominator + weight_decay * master), 0.0
    )
    first_ref[...] = new_first
    second_ref[...] = new_second

    def pick(i, carry):
        at = pl.ds(pl.multiple_of(table_ref[LIST, i] * ROWS, ROWS), ROWS)
        scratch[pl.ds(pl.multiple_of(i * ROWS, ROWS), ROWS), :] = master_ref[at, :]
        return carry

    lax.fori_loop(0, KEPT, pick, 0, unroll=6)
    copy_ref[...] = scratch[...].astype(BF16)


def final_kernel(*refs):
    table_ref = refs[0]
    pieces = refs[1:17]
    out_ref, weights = refs[17:]
    assemble(pieces, *place_of("dp"), weights)

    def step(s, carry):
        entry = table_ref[RANK, s]
        some = (jnp.zeros((B, B), jnp.int32) + entry) < KEPT
        out_ref[s] = jnp.where(some, weights[jnp.minimum(entry, KEPT - 1)], 0.0).astype(BF16)
        return carry

    lax.fori_loop(0, SLOTS, step, 0, unroll=2)


AXES = ("dp", "tensor")
SWAP = [(i, i ^ 1) for i in range(16)]
UP = [(i, (i + 2) % 16) for i in range(16)]
DOWN = [(i, (i - 2) % 16) for i in range(16)]


def direction(z, core):
    return 1 - 2 * ((z + core) % 2)


def exchange(side):
    out = []
    for z, xh, t in itertools.product(range(ZN), range(2), range(16)):
        other = (z + side * direction(z, t % 2)) % ZN
        out.append(((z * 2 + xh) * 16 + t, (other * 2 + xh) * 16 + t))
    return out


NEAR = exchange(1)
FAR = exchange(-1)


def gather_pieces(shard):
    pieces = [[None, None] for _ in range(ZN)]
    swapped = lax.ppermute(shard, "dp", SWAP)
    up = [shard, swapped]
    down = [shard, swapped]
    pieces[0] = [shard, swapped]
    for step in range(1, 4):
        for j in range(2):
            up[j] = lax.ppermute(up[j], "dp", UP)
            down[j] = lax.ppermute(down[j], "dp", DOWN)
        for j in range(2):
            pieces[ZN - step][j] = up[j]
            pieces[step][j] = down[j]
    pieces[4][0] = lax.ppermute(up[0], "dp", UP)
    pieces[4][1] = lax.ppermute(down[1], "dp", DOWN)
    return [piece for pair in pieces for piece in pair]


def y_exchange(side):
    out = []
    for y, xl, core in itertools.product(range(4), range(2), range(2)):
        other = (y + side * direction(y, core)) % 4
        out.append(((y * 2 + xl) * 2 + core, (other * 2 + xl) * 2 + core))
    return out


Y_NEAR = y_exchange(1)
Y_FAR = y_exchange(-1)
X_SWAP = [(i, i ^ 2) for i in range(16)]
CORE_SWAP = [(i, i ^ 1) for i in range(16)]


def hop(value, pairs):
    return lax.ppermute(value, "tensor", pairs)


def reduce_chunks(keep, send):
    got = [lax.ppermute(a, "dp", SWAP) for a in send]
    got = got[:2] + [got[2][:2], got[2][2:]]

    def total(pair, more=None):
        value = keep[pair] + got[pair].astype(F32)
        return (value if more is None else value + more.astype(F32)).astype(BF16)

    a = lax.ppermute(total(0), AXES, FAR)
    b = lax.ppermute(total(1, a), AXES, NEAR)
    c = lax.ppermute(total(2, b), AXES, FAR)
    d = lax.ppermute(total(3, c)[1], AXES, NEAR)
    return keep[3], got[3], c, d


def local(tokens, upstream, master_weights, first_moment, second_moment, old_blocks, new_blocks, new_columns):
    states = [jnp.transpose(a, (1, 0, 2)) for a in (master_weights, first_moment, second_moment)]

    swapped = hop(tokens, X_SWAP)

    table, packed = pl.pallas_call(
        pack_kernel,
        out_shape=(sd((8, 128), jnp.int32), sd((OWNERS * KEEP, ROWS, B), F32)),
        in_specs=[vmem()] * 4,
        out_specs=(vmem(),) * 2,
        scratch_shapes=[pltpu.SMEM((8, 128), jnp.int32), pltpu.SemaphoreType.DMA],
        compiler_params=params(56),
    )(old_blocks, new_blocks, new_columns, states[0])
    arrived = lax.all_to_all(packed, "tensor", split_axis=0, concat_axis=0, tiled=True)

    arrived, swapped = lax.optimization_barrier((arrived, swapped))
    start = jnp.stack([tokens, swapped])
    near = hop(start, Y_NEAR)
    flat = sd((SLOTS * ROWS, B), F32)
    flat16 = sd((KEPT * ROWS, B), BF16)
    copy_in = pl.pallas_call(
        copy_in_kernel,
        out_shape=flat16,
        in_specs=[smem()] + [vmem()] * 2,
        out_specs=vmem(),
        scratch_shapes=[pltpu.VMEM((KEPT * ROWS, B), F32)],
        compiler_params=params(6),
    )(table, states[0], arrived)
    pair = jnp.stack([copy_in, lax.ppermute(copy_in, "dp", SWAP)])
    shards = [pair, lax.ppermute(pair, AXES, NEAR)]
    shards.append(lax.ppermute(jnp.concatenate(shards, axis=0), AXES, FAR))
    shards.append(lax.ppermute(shards[2], AXES, NEAR))
    def after(value, other):
        return lax.optimization_barrier((value, other))[0]

    packed_moments = pl.pallas_call(
        pack_moments_kernel,
        out_shape=sd((OWNERS * KEEP, 2, ROWS, B), F32),
        in_specs=[smem()] + [vmem()] * 2,
        out_specs=vmem(),
        compiler_params=params(56),
    )(table, states[1], states[2])
    shards.append(lax.ppermute(after(shards[3], packed_moments), AXES, FAR))

    far = hop(jnp.concatenate([start, after(near, shards[1])], axis=0), Y_FAR)
    mine = [start, near, after(far, shards[4])]
    token_pieces = mine + [hop(a, CORE_SWAP) for a in mine]

    weights = pl.pallas_call(
        assemble_kernel,
        out_shape=sd((KEPT, B, B), BF16),
        in_specs=[vmem()] * 5,
        out_specs=vmem(),
        scratch_shapes=[pltpu.VMEM((KEPT, B, B), F32)],
        compiler_params=params(12),
    )(*shards)
    moved_moments = lax.all_to_all(
        after(packed_moments, shards[4]), "tensor", split_axis=0, concat_axis=0, tiled=True
    )
    pair32 = sd((2, SLOTS * ROWS, B), F32)
    pair16 = sd((2, SLOTS * ROWS, B), BF16)
    hidden_out, *pairs = pl.pallas_call(
        main_kernel,
        out_shape=(sd(upstream.shape, BF16),) + (pair32,) * 4 + (pair16,) * 2 + (sd((4, SLOTS * ROWS, B), BF16),),
        in_specs=[smem()] + [hbm(), vmem()] + [anywhere()] * 6,
        out_specs=(hbm(),) * 8,
        scratch_shapes=[
            pltpu.VMEM((OWNERS,) + tokens.shape, BF16),
            pltpu.VMEM(upstream.shape, BF16),
            pltpu.VMEM(upstream.shape, BF16),
            pltpu.VMEM((COLS, tokens.shape[0], B), BF16),
            pltpu.VMEM((2 * B, B), F32),
            pltpu.VMEM((ZN, SLOTS * ROWS, B), F32),
            pltpu.VMEM((ZN, SLOTS * ROWS, B), BF16),
            pltpu.SemaphoreType.DMA((OWNERS,)),
            pltpu.SemaphoreType.DMA((2,)),
            pltpu.SemaphoreType.DMA((3, 8)),
        ],
        compiler_params=params(56),
        cost_estimate=pl.CostEstimate(flops=4 * 10**9, bytes_accessed=2 * 10**7, transcendentals=10**6),
    )(table, upstream, weights, *token_pieces)
    keep, send = pairs[:4], pairs[4:]

    moved_moments, keep = lax.optimization_barrier((moved_moments, keep))
    kept_states = pl.pallas_call(
        place_kernel,
        out_shape=(flat,) * 4,
        in_specs=[smem()] + [vmem()] * 5,
        out_specs=(vmem(),) * 4,
        compiler_params=params(8),
    )(table, *states, arrived, moved_moments)

    grads = reduce_chunks(keep, send)

    new_master, new_first, new_second, fresh = pl.pallas_call(
        adam_kernel,
        out_shape=(flat, flat, flat, flat16),
        in_specs=[smem()] + [vmem()] * 8,
        out_specs=(vmem(),) * 4,
        scratch_shapes=[pltpu.VMEM((KEPT * ROWS, B), F32)],
        compiler_params=params(8),
    )(table, *grads, *kept_states)

    final = gather_pieces(fresh)
    weight_copy = pl.pallas_call(
        final_kernel,
        out_shape=sd((SLOTS, B, B), BF16),
        in_specs=[smem()] + [vmem()] * 16,
        out_specs=vmem(),
        scratch_shapes=[pltpu.VMEM((KEPT, B, B), F32)],
        compiler_params=params(12),
    )(table, *final)

    def back(a):
        return jnp.transpose(a.reshape(SLOTS, -1, B), (1, 0, 2))

    return (hidden_out, back(new_master), back(new_first), back(new_second), back(weight_copy))


def solution(mesh):
    split = P("dp", "tensor", None)
    return jax.shard_map(
        local,
        mesh=mesh,
        in_specs=(P("dp", "tensor"), P("dp", "tensor"), split, split, split, P(), P(), P()),
        out_specs=(P("dp", "tensor"), split, split, split, P(None, "tensor", None)),
        check_vma=False,
    )
```
